256 devices in a mesh: wide: 32 (over z_lo, y, core), narrow: 8 (over z_hi, x).
Axes of the slice: x: 4, y: 4, z: 8 (z_hi: 2, z_lo: 4; z = z_hi * 4 + z_lo), core: 2. Of those that a mesh axis runs over, the one named last changes fastest.
Arguments:
- pressure: float32 [512, 512, 1024], P(('narrow', 'wide')), may hold values from -6 to 6
- relax_freq: float32 [2], replicated, may hold values from 4 to 64
- relax_depth: float32 [2], replicated, may hold values from 0.1 to 0.6
Outputs:
- advanced: float32 [512, 512, 1024], P(('narrow', 'wide'))
The draws below stay inside these ranges and needn't reach their ends.
All inputs are finite; a program needn't handle non-finite values.
Results may differ from the reference program's by a relative error of at most 0.000084.
Values sent between devices are 32-bit elements; how exact they have to be, the bound alone decides.
A program may use at most 128 MiB of HBM per device.

```python
import math
import jax
import jax.numpy as jnp
from jax import lax

NY = 512
NT = 1024
SUBSTEPS = 3
NX = 512


def shard_levels(rng, shape, shards, smallest, high):
    gain, own = 1.0, jax.random.fold_in(rng, 6)
    for dim, shards_of in shards:
        steps = jnp.exp(jax.random.uniform(jax.random.fold_in(own, dim), (shards_of,), jnp.float32, smallest / len(shards), high / len(shards)))
        gain = gain * jnp.repeat(steps, shape[dim] // shards_of).reshape([-1 if axis == dim else 1 for axis in range(len(shape))])
    return gain


def scatter_about(stream_key, extent, deviation, most, split=(), kind=jnp.bfloat16):
    factor_of = shard_levels(stream_key, extent, split, -0.22, 0.18) if split else 1.0
    entries = jax.random.normal(stream_key, extent, jnp.float32) * deviation * factor_of
    return jnp.minimum(jnp.maximum(entries, -most), most).astype(kind)


def setup_inputs(seed: int = 0) -> dict:
    splits = jax.random.split(jax.random.key(seed), 4)
    return {
        "pressure": scatter_about(splits[0], (NX, NY, NT), 1.0, 6.0, ((0, 256),), jnp.float32),
        "relax_freq": jnp.clip(jnp.exp(jax.random.uniform(splits[1], (2,), jnp.float32, math.log(4.0), math.log(64.0))), 4.0, 64.0),
        "relax_depth": jnp.clip(jnp.exp(jax.random.uniform(splits[2], (2,), jnp.float32, math.log(0.1), math.log(0.6))), 0.1, 0.6),
    }


WAVE_BREAKING = 0.1
RATE_TOP = 0.2


def burgers(acoustic_signal):
    squared = acoustic_signal * acoustic_signal
    bordered_signal = jnp.pad(squared, [(0, 0)] * (acoustic_signal.ndim - 1) + [(1, 1)])
    return acoustic_signal + WAVE_BREAKING * 0.25 * (bordered_signal[..., 2:] - bordered_signal[..., :-2])


def relax_factor(bin_index, relax_freq, relax_depth):
    total_re = jnp.zeros_like(bin_index)
    imaginary_total = jnp.zeros_like(bin_index)
    for process in range(2):
        ratio = bin_index / relax_freq[process]
        scaled = relax_depth[process] / (1.0 + ratio * ratio)
        total_re = total_re + scaled * ratio * ratio
        imaginary_total = imaginary_total + scaled * ratio
    amplitude = jnp.exp(-total_re)
    return amplitude * jnp.cos(imaginary_total), -amplitude * jnp.sin(imaginary_total)


def transverse_laplace(acoustic_signal):
    bordered_signal = jnp.pad(acoustic_signal, 1)
    return bordered_signal[2:, 1:-1] + bordered_signal[:-2, 1:-1] + bordered_signal[1:-1, 2:] + bordered_signal[1:-1, :-2] - 4.0 * acoustic_signal


def reference(pressure, relax_freq, relax_depth):
    n_freq = NT // 2
    bin_index = jnp.arange(n_freq, dtype=jnp.float32)
    factor_re, factor_im = relax_factor(bin_index, relax_freq, relax_depth)

    def forward(row):
        spectrum = jnp.fft.rfft(burgers(row), axis=-1)[:, :n_freq]
        real_part = jnp.real(spectrum)
        imag_part = jnp.imag(spectrum)
        return (real_part * factor_re - imag_part * factor_im, real_part * factor_im + imag_part * factor_re)

    real_part, imag_part = lax.map(forward, pressure)
    real_part = jnp.transpose(real_part, (2, 0, 1))
    imag_part = jnp.transpose(imag_part, (2, 0, 1))
    half_bins = jnp.float32(n_freq // 2)
    bin_rate = RATE_TOP * jnp.minimum(bin_index, 1.0) * jnp.minimum(1.0, half_bins / jnp.maximum(bin_index, 1.0))

    def diffract(item):
        real_bin, imag_bin, rate = item
        for partial_advance in range(SUBSTEPS):
            real_bin = real_bin - rate * transverse_laplace(imag_bin)
            imag_bin = imag_bin + rate * transverse_laplace(real_bin)
        return real_bin, imag_bin

    real_part, imag_part = lax.map(diffract, (real_part, imag_part, bin_rate))
    real_part = jnp.transpose(real_part, (1, 2, 0))
    imag_part = jnp.transpose(imag_part, (1, 2, 0))

    def inverse(item):
        real_row, imag_row = item
        full = lax.complex(real_row, imag_row)
        bordered_signal = jnp.pad(full, ((0, 0), (0, 1)))
        return jnp.fft.irfft(bordered_signal, n=NT, axis=-1)

    return lax.map(inverse, (real_part, imag_part))
```

```python
import functools

import jax
import jax.numpy as jnp
import ml_dtypes
import numpy as np
from jax import lax
from jax.experimental import pallas as pl
from jax.experimental.pallas import tpu as pltpu
from jax.sharding import PartitionSpec as P

SUBSTEPS = 3
STEPS = 2 * SUBSTEPS
WAVE_BREAKING = 0.1
RATE_TOP = 0.2

NY = 512
NT = 1024
HALF = NT // 2
LANES = 128
CHUNKS = (NT // 2) // LANES
PAD = 8
BLOCK = 256
ROWS = 2
MESH = pl.DeviceIdType.MESH


def chunk_bins(chunk):
    return 2 * (np.arange(LANES) + LANES * (chunk % 2)) + chunk // 2


def split_table(table):
    high = table.astype(ml_dtypes.bfloat16)
    low = (table - high.astype(np.float64)).astype(ml_dtypes.bfloat16)
    return high, low


def forward_tables():
    time = np.arange(HALF)
    tables = []
    for chunk in range(CHUNKS):
        angle = 2.0 * np.pi * (time[:, None] * chunk_bins(chunk)[None, :] % NT) / NT
        tables.append(split_table(np.concatenate([np.cos(angle), -np.sin(angle)], axis=1)))
    return np.stack([np.stack(pair) for pair in tables])


def inverse_tables():
    time = np.arange(HALF)
    tables = []
    for chunk in range(CHUNKS):
        bins = chunk_bins(chunk)
        angle = 2.0 * np.pi * (bins[:, None] * time[None, :] % NT) / NT
        weight = (np.where(bins == 0, 1.0, 2.0) / NT)[:, None]
        parts = []
        for table in (np.cos(angle) * weight, -np.sin(angle) * weight):
            high, low = split_table(table)
            parts.append(np.concatenate([high, high, low], axis=0))
        tables.append(np.stack(parts))
    return np.stack(tables)


def split_values(values):
    high = values.astype(jnp.bfloat16)
    low = (values - high.astype(jnp.float32)).astype(jnp.bfloat16)
    return high, low


def dot(lhs, rhs):
    return jnp.dot(lhs, rhs, preferred_element_type=jnp.float32)


def step_kernel(
    narrow_size, wide_size,
    freq_ref, depth_ref, pressure_ref, forward_ref, inverse_ref,
    out_ref,
    waves, fields, landed, fwd, inv, sums, factors,
    wave_sems, table_sems, out_sems, send_sems, recv_sems,
):
    count = narrow_size * wide_size
    me = lax.axis_index("narrow") * wide_size + lax.axis_index("wide")
    core = lax.rem(me, 2)

    def device(index):
        return {"narrow": index // wide_size, "wide": lax.rem(index, wide_size)}

    def partner(direction):
        return me - 1 + 2 * direction

    def has_partner(direction):
        other = partner(direction)
        return jnp.logical_and(other >= 0, other < count)

    def row_at(turn):
        return lax.rem(core + turn, 2)

    blocks = NY // BLOCK

    def wave_copy(row, block):
        rows = pl.ds(pl.multiple_of(block * BLOCK, BLOCK), BLOCK)
        return pltpu.make_async_copy(
            pressure_ref.at[row, rows], waves.at[row, rows], wave_sems.at[row, block]
        )

    def table_copy(chunk):
        return pltpu.make_async_copy(forward_ref.at[chunk], fwd.at[chunk], table_sems.at[chunk])

    inverse_copy = pltpu.make_async_copy(inverse_ref, inv, table_sems.at[CHUNKS])

    wave_copy(row_at(0), 0).start()
    table_copy(0).start()
    for block in range(1, blocks):
        wave_copy(row_at(0), block).start()
    for chunk in range(1, CHUNKS):
        table_copy(chunk).start()
    for block in range(blocks):
        wave_copy(row_at(1), block).start()
    inverse_copy.start()

    barrier = pltpu.get_barrier_semaphore()
    for direction in range(2):
        @pl.when(has_partner(direction))
        def _():
            pl.semaphore_signal(
                barrier, inc=1, device_id=device(partner(direction)), device_id_type=MESH
            )

    lane = lax.broadcasted_iota(jnp.int32, (8, LANES), 1)
    for chunk in range(CHUNKS):
        bins = (2 * (lane + LANES * (chunk % 2)) + chunk // 2).astype(jnp.float32)
        total_re = jnp.zeros_like(bins)
        total_im = jnp.zeros_like(bins)
        for process in range(2):
            ratio = bins / freq_ref[process]
            scaled = depth_ref[process] / (1.0 + ratio * ratio)
            total_re = total_re + scaled * ratio * ratio
            total_im = total_im + scaled * ratio
        amplitude = jnp.exp(-total_re)
        factors[0, chunk] = amplitude * jnp.cos(total_im)
        factors[1, chunk] = -amplitude * jnp.sin(total_im)
        factors[2, chunk] = (
            RATE_TOP
            * jnp.minimum(bins, 1.0)
            * jnp.minimum(1.0, float(NT // 4) / jnp.maximum(bins, 1.0))
        )

    zero_rows = jnp.zeros((PAD, LANES), jnp.float32)
    for part in range(2):
        for chunk in range(CHUNKS):
            for row in range(ROWS):
                fields[part, chunk, row, 0:PAD] = zero_rows
                fields[part, chunk, row, PAD + NY:] = zero_rows

    pl.semaphore_wait(
        barrier, has_partner(0).astype(jnp.int32) + has_partner(1).astype(jnp.int32)
    )

    def slot(message, direction):
        return 2 * message + direction

    def send(message, part, chunk, direction, start=0, size=NY):
        return pltpu.make_async_remote_copy(
            src_ref=fields.at[part, chunk, direction, pl.ds(PAD + start, size)],
            dst_ref=landed.at[slot(message, direction), pl.ds(start, size)],
            send_sem=send_sems.at[message, direction],
            recv_sem=recv_sems.at[message, direction],
            device_id=device(partner(direction)),
            device_id_type=MESH,
        )

    def forward_block(row, block):
        rows = pl.ds(pl.multiple_of(block * BLOCK, BLOCK), BLOCK)
        inner = pl.ds(pl.multiple_of(PAD + block * BLOCK, PAD), BLOCK)
        wave_copy(row, block).wait()
        wave = waves[row, rows]
        squared = wave * wave
        time = lax.broadcasted_iota(jnp.int32, (BLOCK, NT), 1)
        after = jnp.where(time == NT - 1, 0.0, pltpu.roll(squared, NT - 1, 1))
        before = jnp.where(time == 0, 0.0, pltpu.roll(squared, 1, 1))
        steep = wave + WAVE_BREAKING * 0.25 * (after - before)
        first, second = steep[:, :HALF], steep[:, HALF:]
        pairs = (split_values(first + second), split_values(first - second))
        for chunk in range(CHUNKS):
            high, low = pairs[chunk // 2]
            both = (
                dot(high, fwd[chunk, 0]) + dot(low, fwd[chunk, 0]) + dot(high, fwd[chunk, 1])
            )
            re, im = both[:, :LANES], both[:, LANES:]
            factor_re = factors[0, chunk, 0:1]
            factor_im = factors[1, chunk, 0:1]
            fields[0, chunk, row, inner] = re * factor_re - im * factor_im
            fields[1, chunk, row, inner] = re * factor_im + im * factor_re

    for chunk in range(CHUNKS):
        table_copy(chunk).wait()

    def forward_row(turn, carry):
        row = row_at(turn)

        def one(block, inner_carry):
            forward_block(row, block)

            return inner_carry

        lax.fori_loop(0, blocks, one, 0)

        @pl.when(has_partner(row))
        def _():
            for chunk in range(CHUNKS):
                send(chunk, 1, chunk, row).start()

        return carry

    lax.fori_loop(0, 2, forward_row, 0)

    @pl.when(jnp.logical_or(me == 0, me == count - 1))
    def _():
        landed[2 * STEPS * CHUNKS] = jnp.zeros((NY, LANES), jnp.float32)

    sums[...] = jnp.zeros_like(sums)

    def half_step(message, part, chunk, row):
        halo_from = 1 - row
        at = jnp.where(has_partner(row), slot(message, halo_from), 2 * STEPS * CHUNKS)
        other = 1 - part
        sign = (2 * part - 1).astype(jnp.float32)
        rate = factors[2, chunk, 0:1] * sign
        size = 64
        for start in range(0, NY, size):
            base = PAD + start
            center = fields[other, chunk, row, base:base + size]
            below = fields[other, chunk, row, base - 1:base - 1 + size]
            above = fields[other, chunk, row, base + 1:base + 1 + size]
            beside = fields[other, chunk, 1 - row, base:base + size]
            halo = landed[at, start:start + size]
            laplacian = (halo + beside) + (below + above) - 4.0 * center
            fields[part, chunk, row, base:base + size] += rate * laplacian

    def wait_for(message, part, chunk):
        for direction in range(2):
            @pl.when(has_partner(1 - direction))
            def _():
                send(message, 1 - part, chunk, direction).wait_recv()

    def wait_sent(message, part, chunk):
        for direction in range(2):
            @pl.when(has_partner(direction))
            def _():
                send(message, 1 - part, chunk, direction).wait_send()

    def advance(message, carry):
        step = message // CHUNKS
        chunk = lax.rem(message, CHUNKS)
        part = lax.rem(step, 2)
        wait_for(message, part, chunk)

        @pl.when(step > 0)
        def _():
            wait_sent(message - CHUNKS, 1 - part, chunk)

        for turn in range(2):
            row = row_at(turn)
            half_step(message, part, chunk, row)

            @pl.when(jnp.logical_and(has_partner(row), step < STEPS - 1))
            def _():
                send(message + CHUNKS, part, chunk, row).start()

        @pl.when(step >= STEPS - 2)
        def _():
            for row in range(ROWS):
                def gather(block, inner_carry):
                    inner = pl.ds(pl.multiple_of(PAD + block * BLOCK, PAD), BLOCK)
                    rows = pl.ds(pl.multiple_of(block * BLOCK, BLOCK), BLOCK)
                    high, low = split_values(fields[part, chunk, row, inner])
                    terms = jnp.concatenate([high, low, high], axis=1)
                    sums[chunk // 2, row, rows] += dot(terms, inv[chunk, part])
                    return inner_carry

                lax.fori_loop(0, blocks, gather, 0)

        return carry

    inverse_copy.wait()
    lax.fori_loop(0, STEPS * CHUNKS, advance, 0)

    def out_copy(row, block, side):
        rows = pl.ds(pl.multiple_of(block * BLOCK, BLOCK), BLOCK)
        return pltpu.make_async_copy(
            sums.at[side, row, rows],
            out_ref.at[row, rows, pl.ds(side * HALF, HALF)],
            out_sems.at[row, block, side],
        )

    for row in range(ROWS):
        for block in range(blocks):
            rows = slice(block * BLOCK, (block + 1) * BLOCK)
            even, odd = sums[0, row, rows], sums[1, row, rows]
            sums[0, row, rows] = even + odd
            sums[1, row, rows] = even - odd
            for side in range(2):
                out_copy(row, block, side).start()
    for row in range(ROWS):
        for block in range(blocks):
            for side in range(2):
                out_copy(row, block, side).wait()
    for chunk in range(CHUNKS):
        wait_sent((STEPS - 1) * CHUNKS + chunk, 1, chunk)


def shards(narrow_size, wide_size, pressure, relax_freq, relax_depth):
    blocks = NY // BLOCK
    messages = STEPS * CHUNKS
    hbm = pl.BlockSpec(memory_space=pltpu.HBM)
    smem = pl.BlockSpec(memory_space=pltpu.SMEM)
    f32, bf16 = jnp.float32, jnp.bfloat16
    dma = pltpu.SemaphoreType.DMA
    return pl.pallas_call(
        functools.partial(step_kernel, narrow_size, wide_size),
        out_shape=jax.ShapeDtypeStruct((ROWS, NY, NT), f32),
        in_specs=[smem, smem, hbm, hbm, hbm],
        out_specs=hbm,
        scratch_shapes=[
            pltpu.VMEM((ROWS, NY, NT), f32),
            pltpu.VMEM((2, CHUNKS, ROWS, NY + 2 * PAD, LANES), f32),
            pltpu.VMEM((2 * messages + 1, NY, LANES), f32),
            pltpu.VMEM((CHUNKS, 2, HALF, 2 * LANES), bf16),
            pltpu.VMEM((CHUNKS, 2, 3 * LANES, HALF), bf16),
            pltpu.VMEM((2, ROWS, NY, HALF), f32),
            pltpu.VMEM((3, CHUNKS, 8, LANES), f32),
            dma((ROWS, blocks)),
            dma((CHUNKS + 1,)),
            dma((ROWS, blocks, 2)),
            dma((messages, 2)),
            dma((messages, 2)),
        ],
        compiler_params=pltpu.CompilerParams(
            collective_id=0, has_side_effects=True, vmem_limit_bytes=56 * 2**20
        ),
        cost_estimate=pl.CostEstimate(
            flops=2 * 2 * 3 * ROWS * NY * HALF * NT, bytes_accessed=14 * 2**20, transcendentals=0
        ),
    )(relax_freq, relax_depth, pressure, jnp.asarray(forward_tables()), jnp.asarray(inverse_tables()))


def solution(mesh):
    placed = (P(("narrow", "wide"), None, None), P(), P())
    return jax.shard_map(
        functools.partial(shards, mesh.shape["narrow"], mesh.shape["wide"]),
        mesh=mesh,
        in_specs=placed,
        out_specs=P(("narrow", "wide"), None, None),
        check_vma=False,
    )
```

```python
import functools

import jax
import jax.numpy as jnp
import ml_dtypes
import numpy as np
from jax import lax
from jax.experimental import pallas as pl
from jax.experimental.pallas import tpu as pltpu
from jax.sharding import PartitionSpec as P

SUBSTEPS = 3
STEPS = 2 * SUBSTEPS
WAVE_BREAKING = 0.1
RATE_TOP = 0.2

NY = 512
NT = 1024
HALF = NT // 2
LANES = 128
CHUNKS = (NT // 2) // LANES
PAD = 8
BLOCK = 128
GATHER = 256
PIECES = 4
EAGER = 2
ROWS = 2
MESH = pl.DeviceIdType.MESH


def chunk_bins(chunk):
    return 2 * (np.arange(LANES) + LANES * (chunk % 2)) + chunk // 2


def split_table(table):
    high = table.astype(ml_dtypes.bfloat16)
    low = (table - high.astype(np.float64)).astype(ml_dtypes.bfloat16)
    return high, low


def forward_tables():
    time = np.arange(HALF)
    tables = []
    for chunk in range(CHUNKS):
        angle = 2.0 * np.pi * (time[:, None] * chunk_bins(chunk)[None, :] % NT) / NT
        tables.append(split_table(np.concatenate([np.cos(angle), -np.sin(angle)], axis=1)))
    return np.stack([np.stack(pair) for pair in tables])


def inverse_tables():
    time = np.arange(HALF)
    tables = []
    for chunk in range(CHUNKS):
        bins = chunk_bins(chunk)
        angle = 2.0 * np.pi * (bins[:, None] * time[None, :] % NT) / NT
        weight = (np.where(bins == 0, 1.0, 2.0) / NT)[:, None]
        parts = []
        for table in (np.cos(angle) * weight, -np.sin(angle) * weight):
            high, low = split_table(table)
            parts.append(np.concatenate([high, high, low], axis=0))
        tables.append(np.stack(parts))
    return np.stack(tables)


def split_values(values):
    high = values.astype(jnp.bfloat16)
    low = (values - high.astype(jnp.float32)).astype(jnp.bfloat16)
    return high, low


def dot(lhs, rhs):
    return jnp.dot(lhs, rhs, preferred_element_type=jnp.float32)


def step_kernel(
    narrow_size, wide_size,
    freq_ref, depth_ref, pressure_ref, forward_ref, inverse_ref,
    out_ref,
    waves, fields, landed, fwd, inv, factors,
    wave_sems, table_sems, send_sems, recv_sems, last_send_sems, last_recv_sems,
):
    count = narrow_size * wide_size
    me = lax.axis_index("narrow") * wide_size + lax.axis_index("wide")
    core = lax.rem(me, 2)

    def device(index):
        return {"narrow": index // wide_size, "wide": lax.rem(index, wide_size)}

    def partner(direction):
        return me - 1 + 2 * direction

    def has_partner(direction):
        other = partner(direction)
        return jnp.logical_and(other >= 0, other < count)

    def row_at(turn):
        return lax.rem(core + turn, 2)

    blocks = NY // BLOCK

    def wave_copy(row, block):
        rows = pl.ds(pl.multiple_of(block * BLOCK, BLOCK), BLOCK)
        return pltpu.make_async_copy(
            pressure_ref.at[row, rows], waves.at[row, rows], wave_sems.at[row, block]
        )

    def table_copy(chunk):
        return pltpu.make_async_copy(forward_ref.at[chunk], fwd.at[chunk], table_sems.at[chunk])

    inverse_copy = pltpu.make_async_copy(inverse_ref, inv, table_sems.at[CHUNKS])

    wave_copy(row_at(0), 0).start()
    table_copy(0).start()
    for block in range(1, blocks):
        wave_copy(row_at(0), block).start()
    for chunk in range(1, CHUNKS):
        table_copy(chunk).start()
    for block in range(blocks):
        wave_copy(row_at(1), block).start()
    inverse_copy.start()

    barrier = pltpu.get_barrier_semaphore()
    for direction in range(2):
        @pl.when(has_partner(direction))
        def _():
            pl.semaphore_signal(
                barrier, inc=1, device_id=device(partner(direction)), device_id_type=MESH
            )

    lane = lax.broadcasted_iota(jnp.int32, (8, LANES), 1)
    for chunk in range(CHUNKS):
        bins = (2 * (lane + LANES * (chunk % 2)) + chunk // 2).astype(jnp.float32)
        total_re = jnp.zeros_like(bins)
        total_im = jnp.zeros_like(bins)
        for process in range(2):
            ratio = bins / freq_ref[process]
            scaled = depth_ref[process] / (1.0 + ratio * ratio)
            total_re = total_re + scaled * ratio * ratio
            total_im = total_im + scaled * ratio
        amplitude = jnp.exp(-total_re)
        factors[0, chunk] = amplitude * jnp.cos(total_im)
        factors[1, chunk] = -amplitude * jnp.sin(total_im)
        factors[2, chunk] = (
            RATE_TOP
            * jnp.minimum(bins, 1.0)
            * jnp.minimum(1.0, float(NT // 4) / jnp.maximum(bins, 1.0))
        )

    zero_rows = jnp.zeros((PAD, LANES), jnp.float32)
    for part in range(2):
        for chunk in range(CHUNKS):
            for row in range(ROWS):
                fields[part, chunk, row, 0:PAD] = zero_rows
                fields[part, chunk, row, PAD + NY:] = zero_rows

    pl.semaphore_wait(
        barrier, has_partner(0).astype(jnp.int32) + has_partner(1).astype(jnp.int32)
    )

    def slot(message, direction):
        return 2 * message + direction

    def send(message, part, chunk, direction, start=0, size=NY):
        return pltpu.make_async_remote_copy(
            src_ref=fields.at[part, chunk, direction, pl.ds(PAD + start, size)],
            dst_ref=landed.at[slot(message, direction), pl.ds(start, size)],
            send_sem=send_sems.at[message, direction],
            recv_sem=recv_sems.at[message, direction],
            device_id=device(partner(direction)),
            device_id_type=MESH,
        )

    def forward_block(row, block, first):
        rows = pl.ds(pl.multiple_of(block * BLOCK, BLOCK), BLOCK)
        inner = pl.ds(pl.multiple_of(PAD + block * BLOCK, PAD), BLOCK)
        wave_copy(row, block).wait()
        wave = waves[row, rows]
        squared = wave * wave
        time = lax.broadcasted_iota(jnp.int32, (BLOCK, NT), 1)
        after = jnp.where(time == NT - 1, 0.0, pltpu.roll(squared, NT - 1, 1))
        before = jnp.where(time == 0, 0.0, pltpu.roll(squared, 1, 1))
        steep = wave + WAVE_BREAKING * 0.25 * (after - before)
        early, late = steep[:, :HALF], steep[:, HALF:]
        pairs = (split_values(early + late), split_values(early - late))
        for chunk in range(CHUNKS):
            if first:
                table_copy(chunk).wait()
            high, low = pairs[chunk // 2]
            both = (
                dot(high, fwd[chunk, 0]) + dot(low, fwd[chunk, 0]) + dot(high, fwd[chunk, 1])
            )
            re, im = both[:, :LANES], both[:, LANES:]
            factor_re = factors[0, chunk, 0:1]
            factor_im = factors[1, chunk, 0:1]
            fields[1, chunk, row, inner] = re * factor_im + im * factor_re
            if chunk < EAGER:
                @pl.when(has_partner(row))
                def _():
                    send(chunk, 1, chunk, row, block * BLOCK, BLOCK).start()
            fields[0, chunk, row, inner] = re * factor_re - im * factor_im

    def forward_row(row, first):
        if first:
            forward_block(row, 0, True)

        def one(block, carry):
            forward_block(row, block, False)
            return carry

        lax.fori_loop(1 if first else 0, blocks, one, 0)

        @pl.when(has_partner(row))
        def _():
            for chunk in range(EAGER, CHUNKS):
                send(chunk, 1, chunk, row).start()

    forward_row(row_at(0), True)
    forward_row(row_at(1), False)

    @pl.when(jnp.logical_or(me == 0, me == count - 1))
    def _():
        landed[2 * STEPS * CHUNKS] = jnp.zeros((NY, LANES), jnp.float32)

    def half_step(message, part, chunk, row, first_row=0, count_rows=NY):
        halo_from = 1 - row
        at = jnp.where(has_partner(row), slot(message, halo_from), 2 * STEPS * CHUNKS)
        other = 1 - part
        sign = jnp.float32(2 * part - 1)
        rate = factors[2, chunk, 0:1] * sign
        size = 64
        for start in range(first_row, first_row + count_rows, size):
            base = PAD + start
            center = fields[other, chunk, row, base:base + size]
            below = fields[other, chunk, row, base - 1:base - 1 + size]
            above = fields[other, chunk, row, base + 1:base + 1 + size]
            beside = fields[other, chunk, 1 - row, base:base + size]
            halo = landed[at, start:start + size]
            laplacian = (halo + beside) + (below + above) - 4.0 * center
            fields[part, chunk, row, base:base + size] += rate * laplacian

    def wait_for(message, part, chunk, row):
        @pl.when(has_partner(row))
        def _():
            send(message, 1 - part, chunk, 1 - row).wait_recv()

    def wait_sent(message, part, chunk, direction):
        @pl.when(has_partner(direction))
        def _():
            send(message, 1 - part, chunk, direction).wait_send()

    def terms_of(part, chunk, row, start, size):
        high, low = split_values(fields[part, chunk, row, pl.ds(PAD + start, size)])
        return dot(jnp.concatenate([high, low, high], axis=1), inv[chunk, part])

    def gather(part, chunk, fresh):
        for row in range(ROWS):
            for start in range(0, NY, GATHER):
                terms = terms_of(part, chunk, row, start, GATHER)
                rows = slice(start, start + GATHER)
                side = slice(0, HALF) if chunk < CHUNKS // 2 else slice(HALF, NT)
                if fresh:
                    out_ref[row, rows, side] = terms
                else:
                    out_ref[row, rows, side] += terms

    def advance(message, carry):
        step = message // CHUNKS
        chunk = lax.rem(message, CHUNKS)
        part = lax.rem(step, 2)

        @pl.when(step > 0)
        def _():
            for direction in range(2):
                wait_sent(message - CHUNKS, 1 - part, chunk, direction)

        for turn in range(2):
            row = row_at(turn)
            wait_for(message, part, chunk, row)
            half_step(message, part, chunk, row)

            @pl.when(has_partner(row))
            def _():
                send(message + CHUNKS, part, chunk, row).start()

        return carry

    lax.fori_loop(0, (STEPS - 2) * CHUNKS, advance, 0)
    inverse_copy.wait()

    piece_rows = NY // PIECES
    last = STEPS * CHUNKS - 1

    def piece_copy(piece, direction):
        start = piece * piece_rows
        return pltpu.make_async_remote_copy(
            src_ref=fields.at[0, CHUNKS - 1, direction, pl.ds(PAD + start, piece_rows)],
            dst_ref=landed.at[slot(last, direction), pl.ds(start, piece_rows)],
            send_sem=last_send_sems.at[piece],
            recv_sem=last_recv_sems.at[piece],
            device_id=device(partner(direction)),
            device_id_type=MESH,
        )

    leaving, staying = row_at(0), row_at(1)

    for chunk in range(CHUNKS):
        message = (STEPS - 2) * CHUNKS + chunk
        for direction in range(2):
            wait_sent(message - CHUNKS, 1, chunk, direction)
        wait_for(message, 0, chunk, leaving)
        if chunk < CHUNKS - 1:
            half_step(message, 0, chunk, leaving)

            @pl.when(has_partner(leaving))
            def _():
                send(message + CHUNKS, 0, chunk, leaving).start()
        else:
            for piece in range(PIECES):
                half_step(message, 0, chunk, leaving, piece * piece_rows, piece_rows)

                @pl.when(has_partner(leaving))
                def _():
                    piece_copy(piece, leaving).start()
        wait_for(message, 0, chunk, staying)
        half_step(message, 0, chunk, staying)

        @pl.when(has_partner(staying))
        def _():
            send(message + CHUNKS, 0, chunk, staying).start()

        gather(0, chunk, chunk % 2 == 0)

    for chunk in range(CHUNKS - 1):
        message = (STEPS - 1) * CHUNKS + chunk
        for direction in range(2):
            wait_sent(message - CHUNKS, 0, chunk, direction)
        for row in (staying, leaving):
            wait_for(message, 1, chunk, row)
            half_step(message, 1, chunk, row)
        gather(1, chunk, False)

    def combine(row, rows):
        even, odd = out_ref[row, rows, :HALF], out_ref[row, rows, HALF:]
        out_ref[row, rows, :HALF] = even + odd
        out_ref[row, rows, HALF:] = even - odd

    for row in range(ROWS):
        for start in range(0, NY, 64):
            combine(row, slice(start, start + 64))

    def finish(row, start, size):
        half_step(last, 1, CHUNKS - 1, row, start, size)
        terms = terms_of(1, CHUNKS - 1, row, start, size)
        rows = slice(start, start + size)
        out_ref[row, rows, :HALF] += terms
        out_ref[row, rows, HALF:] -= terms

    for direction in range(2):
        wait_sent(last - CHUNKS, 0, CHUNKS - 1, direction)
    wait_for(last, 1, CHUNKS - 1, staying)
    for start in range(0, NY, GATHER):
        finish(staying, start, GATHER)
    for piece in range(PIECES):
        @pl.when(has_partner(leaving))
        def _():
            piece_copy(piece, 1 - leaving).wait_recv()

        finish(leaving, piece * piece_rows, piece_rows)

    for chunk in range(CHUNKS):
        message = (STEPS - 1) * CHUNKS + chunk
        wait_sent(message, 1, chunk, staying)
        if chunk < CHUNKS - 1:
            wait_sent(message, 1, chunk, leaving)
    for piece in range(PIECES):
        @pl.when(has_partner(leaving))
        def _():
            piece_copy(piece, leaving).wait_send()


def shards(narrow_size, wide_size, pressure, relax_freq, relax_depth):
    blocks = NY // BLOCK
    messages = STEPS * CHUNKS
    hbm = pl.BlockSpec(memory_space=pltpu.HBM)
    smem = pl.BlockSpec(memory_space=pltpu.SMEM)
    f32, bf16 = jnp.float32, jnp.bfloat16
    dma = pltpu.SemaphoreType.DMA
    return pl.pallas_call(
        functools.partial(step_kernel, narrow_size, wide_size),
        out_shape=pltpu.VMEM((ROWS, NY, NT), f32),
        in_specs=[smem, smem, hbm, hbm, hbm],
        out_specs=pl.BlockSpec(memory_space=pltpu.VMEM),
        scratch_shapes=[
            pltpu.VMEM((ROWS, NY, NT), f32),
            pltpu.VMEM((2, CHUNKS, ROWS, NY + 2 * PAD, LANES), f32),
            pltpu.VMEM((2 * messages + 1, NY, LANES), f32),
            pltpu.VMEM((CHUNKS, 2, HALF, 2 * LANES), bf16),
            pltpu.VMEM((CHUNKS, 2, 3 * LANES, HALF), bf16),
            pltpu.VMEM((3, CHUNKS, 8, LANES), f32),
            dma((ROWS, blocks)),
            dma((CHUNKS + 1,)),
            dma((messages, 2)),
            dma((messages, 2)),
            dma((PIECES,)),
            dma((PIECES,)),
        ],
        compiler_params=pltpu.CompilerParams(
            collective_id=0, has_side_effects=True, vmem_limit_bytes=59 * 2**20
        ),
        cost_estimate=pl.CostEstimate(
            flops=2 * 2 * 3 * ROWS * NY * HALF * NT, bytes_accessed=14 * 2**20, transcendentals=0
        ),
    )(relax_freq, relax_depth, pressure, jnp.asarray(forward_tables()), jnp.asarray(inverse_tables()))


def solution(mesh):
    placed = (P(("narrow", "wide"), None, None), P(), P())
    return jax.shard_map(
        functools.partial(shards, mesh.shape["narrow"], mesh.shape["wide"]),
        mesh=mesh,
        in_specs=placed,
        out_specs=P(("narrow", "wide"), None, None),
        check_vma=False,
    )
```

```python
import functools

import jax
import jax.numpy as jnp
import ml_dtypes
import numpy as np
from jax import lax
from jax.experimental import pallas as pl
from jax.experimental.pallas import tpu as pltpu
from jax.sharding import PartitionSpec as P

SUBSTEPS = 3
STEPS = 2 * SUBSTEPS
WAVE_BREAKING = 0.1
RATE_TOP = 0.2

NY = 512
NT = 1024
HALF = NT // 2
LANES = 128
CHUNKS = (NT // 2) // LANES
PAD = 8
LEADING = (96, 416)
TRAILING = (256, 256)
GATHER = 256
PIECES = (384, 128)
EAGER = 4
SLOTS = 2 * CHUNKS
ROWS = 2
MESH = pl.DeviceIdType.MESH


def starts(sizes):
    return [sum(sizes[:index]) for index in range(len(sizes))]


def chunk_bins(chunk):
    return 2 * (np.arange(LANES) + LANES * (chunk % 2)) + chunk // 2


def split_table(table):
    high = table.astype(ml_dtypes.bfloat16)
    low = (table - high.astype(np.float64)).astype(ml_dtypes.bfloat16)
    return high, low


def forward_tables():
    time = np.arange(HALF)
    tables = []
    for chunk in range(CHUNKS):
        angle = 2.0 * np.pi * (time[:, None] * chunk_bins(chunk)[None, :] % NT) / NT
        tables.append(split_table(np.concatenate([np.cos(angle), -np.sin(angle)], axis=1)))
    return np.stack([np.stack(pair) for pair in tables])


def inverse_tables():
    time = np.arange(HALF)
    tables = []
    for chunk in range(CHUNKS):
        bins = chunk_bins(chunk)
        angle = 2.0 * np.pi * (bins[:, None] * time[None, :] % NT) / NT
        weight = (np.where(bins == 0, 1.0, 2.0) / NT)[:, None]
        parts = []
        for table in (np.cos(angle) * weight, -np.sin(angle) * weight):
            high, low = split_table(table)
            parts.append(np.concatenate([high, high, low], axis=0))
        tables.append(np.stack(parts))
    return np.stack(tables)


def split_values(values):
    high = values.astype(jnp.bfloat16)
    low = (values - high.astype(jnp.float32)).astype(jnp.bfloat16)
    return high, low


def dot(lhs, rhs):
    return jnp.dot(lhs, rhs, preferred_element_type=jnp.float32)


def step_kernel(
    narrow_size, wide_size,
    freq_ref, depth_ref, pressure_ref, forward_ref, inverse_ref,
    out_ref,
    waves, fields, landed, fwd, inv, factors, freqs, depths,
    wave_sems, table_sems, scalar_sems, send_sems, recv_sems, last_send_sems, last_recv_sems,
):
    count = narrow_size * wide_size
    me = lax.axis_index("narrow") * wide_size + lax.axis_index("wide")
    core = lax.rem(me, 2)

    def device(index):
        return {"narrow": index // wide_size, "wide": lax.rem(index, wide_size)}

    def partner(direction):
        return me - 1 + 2 * direction

    def has_partner(direction):
        other = partner(direction)
        return jnp.logical_and(other >= 0, other < count)

    def row_at(turn):
        return lax.rem(core + turn, 2)

    def wave_copy(turn, block):
        sizes = (LEADING, TRAILING)[turn]
        rows = pl.ds(starts(sizes)[block], sizes[block])
        return pltpu.make_async_copy(
            pressure_ref.at[row_at(turn), rows],
            waves.at[row_at(turn), rows],
            wave_sems.at[turn * len(LEADING) + block],
        )

    def table_copy(chunk):
        return pltpu.make_async_copy(forward_ref.at[chunk], fwd.at[chunk], table_sems.at[chunk])

    inverse_copy = pltpu.make_async_copy(inverse_ref, inv, table_sems.at[CHUNKS])
    freq_copy = pltpu.make_async_copy(freq_ref, freqs, scalar_sems.at[0])
    depth_copy = pltpu.make_async_copy(depth_ref, depths, scalar_sems.at[1])

    freq_copy.start()
    depth_copy.start()
    wave_copy(0, 0).start()
    table_copy(0).start()
    wave_copy(0, 1).start()
    table_copy(1).start()
    for block in range(2, len(LEADING)):
        wave_copy(0, block).start()
    for chunk in range(2, CHUNKS):
        table_copy(chunk).start()
    for block in range(len(TRAILING)):
        wave_copy(1, block).start()
    barrier = pltpu.get_barrier_semaphore()
    for direction in range(2):
        @pl.when(has_partner(direction))
        def _():
            pl.semaphore_signal(
                barrier, inc=1, device_id=device(partner(direction)), device_id_type=MESH
            )

    lane = lax.broadcasted_iota(jnp.int32, (8, LANES), 1)
    chunk_of = lax.broadcasted_iota(jnp.int32, (8, LANES), 0) & (CHUNKS - 1)
    bins = (2 * (lane + LANES * (chunk_of & 1)) + (chunk_of >> 1)).astype(jnp.float32)
    total_re = jnp.zeros_like(bins)
    total_im = jnp.zeros_like(bins)
    freq_copy.wait()
    depth_copy.wait()
    for process in range(2):
        ratio = bins / freqs[process]
        scaled = depths[process] / (1.0 + ratio * ratio)
        total_re = total_re + scaled * ratio * ratio
        total_im = total_im + scaled * ratio
    amplitude = jnp.exp(-total_re)
    rates = (
        RATE_TOP
        * jnp.minimum(bins, 1.0)
        * jnp.minimum(1.0, float(NT // 4) / jnp.maximum(bins, 1.0))
    )
    table = (amplitude * jnp.cos(total_im), -amplitude * jnp.sin(total_im), rates)
    for kind in range(3):
        for chunk in range(CHUNKS):
            factors[kind, chunk] = jnp.broadcast_to(table[kind][chunk:chunk + 1], (8, LANES))

    zero_rows = jnp.zeros((PAD, LANES), jnp.float32)
    for part in range(2):
        for chunk in range(CHUNKS):
            for row in range(ROWS):
                fields[part, chunk, row, 0:PAD] = zero_rows
                fields[part, chunk, row, PAD + NY:] = zero_rows

    pl.semaphore_wait(
        barrier, has_partner(0).astype(jnp.int32) + has_partner(1).astype(jnp.int32)
    )

    def slot(message, direction):
        return 2 * (message % SLOTS) + direction

    def send(message, part, chunk, direction, start=0, size=NY):
        return pltpu.make_async_remote_copy(
            src_ref=fields.at[part, chunk, direction, pl.ds(PAD + start, size)],
            dst_ref=landed.at[slot(message, direction), pl.ds(start, size)],
            send_sem=send_sems.at[slot(message, direction)],
            recv_sem=recv_sems.at[slot(message, direction)],
            device_id=device(partner(direction)),
            device_id_type=MESH,
        )

    def forward_block(turn, block):
        row = row_at(turn)
        sizes = (LEADING, TRAILING)[turn]
        start, size = starts(sizes)[block], sizes[block]
        rows, inner = pl.ds(start, size), pl.ds(PAD + start, size)
        wave_copy(turn, block).wait()
        wave = waves[row, rows]
        squared = wave * wave
        time = lax.broadcasted_iota(jnp.int32, (size, NT), 1)
        after = jnp.where(time == NT - 1, 0.0, pltpu.roll(squared, NT - 1, 1))
        before = jnp.where(time == 0, 0.0, pltpu.roll(squared, 1, 1))
        steep = wave + WAVE_BREAKING * 0.25 * (after - before)
        early, late = steep[:, :HALF], steep[:, HALF:]
        pairs = (split_values(early + late), split_values(early - late))
        for chunk in range(CHUNKS):
            if turn == 0 and block == 0:
                table_copy(chunk).wait()
            high, low = pairs[chunk // 2]
            both = (
                dot(high, fwd[chunk, 0]) + dot(low, fwd[chunk, 0]) + dot(high, fwd[chunk, 1])
            )
            re, im = both[:, :LANES], both[:, LANES:]
            factor_re = factors[0, chunk, 0:1]
            factor_im = factors[1, chunk, 0:1]
            fields[1, chunk, row, inner] = re * factor_im + im * factor_re
            if chunk < EAGER and turn == 0:
                @pl.when(has_partner(row))
                def _():
                    send(chunk, 1, chunk, row, start, size).start()
            fields[0, chunk, row, inner] = re * factor_re - im * factor_im

    for turn in range(2):
        for block in range(len((LEADING, TRAILING)[turn])):
            forward_block(turn, block)

        @pl.when(has_partner(row_at(turn)))
        def _():
            for chunk in range(EAGER if turn == 0 else 0, CHUNKS):
                send(chunk, 1, chunk, row_at(turn)).start()

    inverse_copy.start()

    @pl.when(jnp.logical_or(me == 0, me == count - 1))
    def _():
        landed[2 * SLOTS] = jnp.zeros((NY, LANES), jnp.float32)

    def half_step(message, part, chunk, row, first_row=0, count_rows=NY):
        halo_from = 1 - row
        at = jnp.where(has_partner(row), slot(message, halo_from), 2 * SLOTS)
        other = 1 - part
        sign = jnp.float32(2 * part - 1)
        rate = factors[2, chunk, 0:1] * sign
        size = 64
        for start in range(first_row, first_row + count_rows, size):
            base = PAD + start
            center = fields[other, chunk, row, base:base + size]
            below = fields[other, chunk, row, base - 1:base - 1 + size]
            above = fields[other, chunk, row, base + 1:base + 1 + size]
            beside = fields[other, chunk, 1 - row, base:base + size]
            halo = landed[at, start:start + size]
            laplacian = (halo + beside) + (below + above) - 4.0 * center
            fields[part, chunk, row, base:base + size] += rate * laplacian

    def wait_for(message, part, chunk, row):
        @pl.when(has_partner(row))
        def _():
            send(message, 1 - part, chunk, 1 - row).wait_recv()

    def wait_sent(message, part, chunk, direction):
        @pl.when(has_partner(direction))
        def _():
            send(message, 1 - part, chunk, direction).wait_send()

    def terms_of(part, chunk, row, start, size):
        high, low = split_values(fields[part, chunk, row, pl.ds(PAD + start, size)])
        return dot(jnp.concatenate([high, low, high], axis=1), inv[chunk, part])

    def gather(part, chunk, row, start, size, fresh=False, combined=False):
        terms = terms_of(part, chunk, row, start, size)
        rows = slice(start, start + size)
        side = slice(0, HALF) if chunk < CHUNKS // 2 else slice(HALF, NT)
        if fresh:
            out_ref[row, rows, side] = terms
        elif combined:
            out_ref[row, rows, :HALF] += terms
            out_ref[row, rows, HALF:] -= terms
        else:
            out_ref[row, rows, side] += terms

    def gather_rows(part, chunk, **kind):
        for row in range(ROWS):
            for start in range(0, NY, GATHER):
                gather(part, chunk, row, start, GATHER, **kind)

    def advance(message, carry):
        step = message // CHUNKS
        chunk = lax.rem(message, CHUNKS)
        part = lax.rem(step, 2)

        @pl.when(step > 0)
        def _():
            for direction in range(2):
                wait_sent(message - CHUNKS, 1 - part, chunk, direction)

        for turn in range(2):
            row = row_at(turn)
            wait_for(message, part, chunk, row)
            half_step(message, part, chunk, row)

            @pl.when(has_partner(row))
            def _():
                send(message + CHUNKS, part, chunk, row).start()

        return carry

    lax.fori_loop(0, (STEPS - 2) * CHUNKS, advance, 0)
    inverse_copy.wait()

    last = STEPS * CHUNKS - 1

    def piece_copy(piece, direction):
        start, piece_rows = starts(PIECES)[piece], PIECES[piece]
        return pltpu.make_async_remote_copy(
            src_ref=fields.at[0, CHUNKS - 1, direction, pl.ds(PAD + start, piece_rows)],
            dst_ref=landed.at[slot(last, direction), pl.ds(start, piece_rows)],
            send_sem=last_send_sems.at[piece],
            recv_sem=last_recv_sems.at[piece],
            device_id=device(partner(direction)),
            device_id_type=MESH,
        )

    leaving, staying = row_at(0), row_at(1)

    for chunk in range(CHUNKS):
        message = (STEPS - 2) * CHUNKS + chunk
        for direction in range(2):
            wait_sent(message - CHUNKS, 1, chunk, direction)
        wait_for(message, 0, chunk, leaving)
        if chunk < CHUNKS - 1:
            half_step(message, 0, chunk, leaving)

            @pl.when(has_partner(leaving))
            def _():
                send(message + CHUNKS, 0, chunk, leaving).start()
        else:
            for piece in range(len(PIECES)):
                half_step(message, 0, chunk, leaving, starts(PIECES)[piece], PIECES[piece])

                @pl.when(has_partner(leaving))
                def _():
                    piece_copy(piece, leaving).start()
        wait_for(message, 0, chunk, staying)
        half_step(message, 0, chunk, staying)

        @pl.when(has_partner(staying))
        def _():
            send(message + CHUNKS, 0, chunk, staying).start()

        gather_rows(0, chunk, fresh=chunk % 2 == 0)

    def combine(row, rows):
        even, odd = out_ref[row, rows, :HALF], out_ref[row, rows, HALF:]
        out_ref[row, rows, :HALF] = even + odd
        out_ref[row, rows, HALF:] = even - odd

    for chunk in range(CHUNKS - 1):
        message = (STEPS - 1) * CHUNKS + chunk
        for direction in range(2):
            wait_sent(message - CHUNKS, 0, chunk, direction)
        for row in (staying, leaving):
            wait_for(message, 1, chunk, row)
            half_step(message, 1, chunk, row)
        gather_rows(1, chunk, combined=chunk >= CHUNKS // 2)
        if chunk == CHUNKS // 2 - 1:
            for row in range(ROWS):
                for start in range(0, NY, 64):
                    combine(row, slice(start, start + 64))

    def finish(row, start, size):
        half_step(last, 1, CHUNKS - 1, row, start, size)
        gather(1, CHUNKS - 1, row, start, size, combined=True)

    for direction in range(2):
        wait_sent(last - CHUNKS, 0, CHUNKS - 1, direction)
    wait_for(last, 1, CHUNKS - 1, staying)
    for start in range(0, NY, GATHER):
        finish(staying, start, GATHER)
    for piece in range(len(PIECES)):
        @pl.when(has_partner(leaving))
        def _():
            piece_copy(piece, 1 - leaving).wait_recv()

        finish(leaving, starts(PIECES)[piece], PIECES[piece])

    for chunk in range(CHUNKS):
        message = (STEPS - 1) * CHUNKS + chunk
        wait_sent(message, 1, chunk, staying)
        if chunk < CHUNKS - 1:
            wait_sent(message, 1, chunk, leaving)
    for piece in range(len(PIECES)):
        @pl.when(has_partner(leaving))
        def _():
            piece_copy(piece, leaving).wait_send()


def shards(narrow_size, wide_size, pressure, relax_freq, relax_depth):
    hbm = pl.BlockSpec(memory_space=pltpu.HBM)
    f32, bf16 = jnp.float32, jnp.bfloat16
    dma = pltpu.SemaphoreType.DMA
    return pl.pallas_call(
        functools.partial(step_kernel, narrow_size, wide_size),
        out_shape=pltpu.VMEM((ROWS, NY, NT), f32),
        in_specs=[hbm, hbm, hbm, hbm, hbm],
        out_specs=pl.BlockSpec(memory_space=pltpu.VMEM),
        scratch_shapes=[
            pltpu.VMEM((ROWS, NY, NT), f32),
            pltpu.VMEM((2, CHUNKS, ROWS, NY + 2 * PAD, LANES), f32),
            pltpu.VMEM((2 * SLOTS + 1, NY, LANES), f32),
            pltpu.VMEM((CHUNKS, 2, HALF, 2 * LANES), bf16),
            pltpu.VMEM((CHUNKS, 2, 3 * LANES, HALF), bf16),
            pltpu.VMEM((3, CHUNKS, 8, LANES), f32),
            pltpu.SMEM((2,), f32),
            pltpu.SMEM((2,), f32),
            dma((len(LEADING) + len(TRAILING),)),
            dma((CHUNKS + 1,)),
            dma((2,)),
            dma((2 * SLOTS,)),
            dma((2 * SLOTS,)),
            dma((len(PIECES),)),
            dma((len(PIECES),)),
        ],
        compiler_params=pltpu.CompilerParams(
            collective_id=0, has_side_effects=True, vmem_limit_bytes=59 * 2**20
        ),
        cost_estimate=pl.CostEstimate(
            flops=2 * 2 * 3 * ROWS * NY * HALF * NT, bytes_accessed=14 * 2**20, transcendentals=0
        ),
    )(relax_freq, relax_depth, pressure, jnp.asarray(forward_tables()), jnp.asarray(inverse_tables()))


def solution(mesh):
    placed = (P(("narrow", "wide"), None, None), P(), P())
    return jax.shard_map(
        functools.partial(shards, mesh.shape["narrow"], mesh.shape["wide"]),
        mesh=mesh,
        in_specs=placed,
        out_specs=P(("narrow", "wide"), None, None),
        check_vma=False,
    )
```

```python
import functools
import math

import jax
import jax.numpy as jnp
import ml_dtypes
import numpy as np
from jax import lax
from jax.experimental import pallas as pl
from jax.experimental.pallas import tpu as pltpu
from jax.sharding import PartitionSpec as P

SUBSTEPS = 3
STEPS = 2 * SUBSTEPS
WAVE_BREAKING = 0.1
RATE_TOP = 0.2

NY = 512
NT = 1024
HALF = NT // 2
LANES = 128
CHUNKS = (NT // 2) // LANES
PAD = 8
LEADING = (96, 416)
TRAILING = (256, 256)
GATHER = 256
PIECES = (384, 128)
EAGER = 4
SLOTS = 2 * CHUNKS
ROWS = 2
MESH = pl.DeviceIdType.MESH
ROOT_HALF = math.sqrt(0.5)


def starts(sizes):
    return [sum(sizes[:index]) for index in range(len(sizes))]


def chunk_bins(chunk):
    lane = np.arange(LANES)
    if chunk < 2:
        return 4 * lane + 2 * chunk, np.ones(LANES)
    bins = 8 * lane + 1 + 4 * (chunk - 2)
    mirrored = bins > HALF
    return np.where(mirrored, NT - bins, bins), np.where(mirrored, -1.0, 1.0)


def chunk_table(chunk):
    bins, sign = chunk_bins(chunk)
    at = np.where(sign < 0, NT - bins, bins)
    time = np.arange(2 * LANES if chunk < 2 else LANES)
    angle = 2.0 * np.pi * (time[:, None] * at[None, :] % NT) / NT
    cosine, sine = np.cos(angle), np.sin(angle)
    if chunk < 2:
        return np.concatenate([cosine, -sine], axis=1)
    return np.concatenate(
        [
            np.concatenate([cosine, -sine * sign], axis=1),
            np.concatenate([-sine, -cosine * sign], axis=1),
        ],
        axis=0,
    )


def split_table(table):
    high = table.astype(ml_dtypes.bfloat16)
    low = (table - high.astype(np.float64)).astype(ml_dtypes.bfloat16)
    return high, low


def forward_tables():
    return np.stack([np.stack(split_table(chunk_table(chunk))) for chunk in range(CHUNKS)])


def inverse_tables():
    tables = []
    for chunk in range(CHUNKS):
        weight = (np.where(chunk_bins(chunk)[0] == 0, 1.0, 2.0) / NT)[:, None]
        parts = []
        for part in range(2):
            columns = slice(part * LANES, (part + 1) * LANES)
            high, low = split_table(chunk_table(chunk)[:, columns].T * weight)
            parts.append(np.concatenate([high, high, low], axis=0))
        tables.append(np.stack(parts))
    return np.stack(tables)


def fold(groups):
    u = [groups[index] + groups[index + 4] for index in range(4)]
    v = [groups[index] - groups[index + 4] for index in range(4)]
    across = (v[1] - v[3]) * ROOT_HALF
    along = (v[1] + v[3]) * ROOT_HALF
    return (
        (u[0] + u[2], u[1] + u[3]),
        (u[0] - u[2], u[1] - u[3]),
        (v[0] + across, v[2] + along),
        (v[0] - across, v[2] - along),
    )


def unfold(sums):
    (a0, a1), (b0, b1), (p0, p1), (q0, q1) = sums
    u = (a0 + b0, a1 + b1, a0 - b0, a1 - b1)
    across, along = p0 - q0, p1 - q1
    v = (p0 + q0, (along + across) * ROOT_HALF, p1 + q1, (along - across) * ROOT_HALF)
    return [u[index] + v[index] for index in range(4)] + [u[index] - v[index] for index in range(4)]


def split_values(values):
    high = values.astype(jnp.bfloat16)
    low = (values - high.astype(jnp.float32)).astype(jnp.bfloat16)
    return high, low


def dot(lhs, rhs):
    return jnp.dot(lhs, rhs, preferred_element_type=jnp.float32)


def step_kernel(
    narrow_size, wide_size,
    freq_ref, depth_ref, pressure_ref, forward_ref, inverse_ref,
    out_ref,
    waves, fields, landed, fwd, inv, factors, freqs, depths,
    wave_sems, table_sems, scalar_sems, send_sems, recv_sems, last_send_sems, last_recv_sems,
):
    count = narrow_size * wide_size
    me = lax.axis_index("narrow") * wide_size + lax.axis_index("wide")
    core = lax.rem(me, 2)

    def device(index):
        return {"narrow": index // wide_size, "wide": lax.rem(index, wide_size)}

    def partner(direction):
        return me - 1 + 2 * direction

    def has_partner(direction):
        other = partner(direction)
        return jnp.logical_and(other >= 0, other < count)

    def row_at(turn):
        return lax.rem(core + turn, 2)

    def wave_copy(turn, block):
        sizes = (LEADING, TRAILING)[turn]
        rows = pl.ds(starts(sizes)[block], sizes[block])
        return pltpu.make_async_copy(
            pressure_ref.at[row_at(turn), rows],
            waves.at[row_at(turn), rows],
            wave_sems.at[turn * len(LEADING) + block],
        )

    def table_copy(chunk):
        return pltpu.make_async_copy(forward_ref.at[chunk], fwd.at[chunk], table_sems.at[chunk])

    inverse_copy = pltpu.make_async_copy(inverse_ref, inv, table_sems.at[CHUNKS])
    freq_copy = pltpu.make_async_copy(freq_ref, freqs, scalar_sems.at[0])
    depth_copy = pltpu.make_async_copy(depth_ref, depths, scalar_sems.at[1])

    freq_copy.start()
    depth_copy.start()
    wave_copy(0, 0).start()
    table_copy(0).start()
    wave_copy(0, 1).start()
    table_copy(1).start()
    for block in range(2, len(LEADING)):
        wave_copy(0, block).start()
    for chunk in range(2, CHUNKS):
        table_copy(chunk).start()
    for block in range(len(TRAILING)):
        wave_copy(1, block).start()
    barrier = pltpu.get_barrier_semaphore()
    for direction in range(2):
        @pl.when(has_partner(direction))
        def _():
            pl.semaphore_signal(
                barrier, inc=1, device_id=device(partner(direction)), device_id_type=MESH
            )

    lane = lax.broadcasted_iota(jnp.int32, (8, LANES), 1)
    chunk_of = lax.broadcasted_iota(jnp.int32, (8, LANES), 0) & (CHUNKS - 1)
    counted = 8 * lane + 4 * chunk_of - 7
    odd = jnp.where(counted > HALF, NT - counted, counted)
    bins = jnp.where(chunk_of < 2, 4 * lane + 2 * chunk_of, odd).astype(jnp.float32)
    total_re = jnp.zeros_like(bins)
    total_im = jnp.zeros_like(bins)
    freq_copy.wait()
    depth_copy.wait()
    for process in range(2):
        ratio = bins / freqs[process]
        scaled = depths[process] / (1.0 + ratio * ratio)
        total_re = total_re + scaled * ratio * ratio
        total_im = total_im + scaled * ratio
    amplitude = jnp.exp(-total_re)
    rates = (
        RATE_TOP
        * jnp.minimum(bins, 1.0)
        * jnp.minimum(1.0, float(NT // 4) / jnp.maximum(bins, 1.0))
    )
    table = (amplitude * jnp.cos(total_im), -amplitude * jnp.sin(total_im), rates)
    for kind in range(3):
        for chunk in range(CHUNKS):
            factors[kind, chunk] = jnp.broadcast_to(table[kind][chunk:chunk + 1], (8, LANES))

    zero_rows = jnp.zeros((PAD, LANES), jnp.float32)
    for part in range(2):
        for chunk in range(CHUNKS):
            for row in range(ROWS):
                fields[part, chunk, row, 0:PAD] = zero_rows
                fields[part, chunk, row, PAD + NY:] = zero_rows

    pl.semaphore_wait(
        barrier, has_partner(0).astype(jnp.int32) + has_partner(1).astype(jnp.int32)
    )

    def slot(message, direction):
        return 2 * (message % SLOTS) + direction

    def send(message, part, chunk, direction, start=0, size=NY):
        return pltpu.make_async_remote_copy(
            src_ref=fields.at[part, chunk, direction, pl.ds(PAD + start, size)],
            dst_ref=landed.at[slot(message, direction), pl.ds(start, size)],
            send_sem=send_sems.at[slot(message, direction)],
            recv_sem=recv_sems.at[slot(message, direction)],
            device_id=device(partner(direction)),
            device_id_type=MESH,
        )

    def forward_block(turn, block):
        row = row_at(turn)
        sizes = (LEADING, TRAILING)[turn]
        start, size = starts(sizes)[block], sizes[block]
        rows, inner = pl.ds(start, size), pl.ds(PAD + start, size)
        wave_copy(turn, block).wait()
        wave = waves[row, rows]
        squared = wave * wave
        time = lax.broadcasted_iota(jnp.int32, (size, NT), 1)
        after = jnp.where(time == NT - 1, 0.0, pltpu.roll(squared, NT - 1, 1))
        before = jnp.where(time == 0, 0.0, pltpu.roll(squared, 1, 1))
        steep = wave + WAVE_BREAKING * 0.25 * (after - before)
        folded = fold([steep[:, at:at + LANES] for at in range(0, NT, LANES)])
        for chunk in range(CHUNKS):
            if turn == 0 and block == 0:
                table_copy(chunk).wait()
            high, low = split_values(jnp.concatenate(folded[chunk], axis=1))
            both = (
                dot(high, fwd[chunk, 0]) + dot(low, fwd[chunk, 0]) + dot(high, fwd[chunk, 1])
            )
            re, im = both[:, :LANES], both[:, LANES:]
            factor_re = factors[0, chunk, 0:1]
            factor_im = factors[1, chunk, 0:1]
            fields[1, chunk, row, inner] = re * factor_im + im * factor_re
            if chunk < EAGER and turn == 0:
                @pl.when(has_partner(row))
                def _():
                    send(chunk, 1, chunk, row, start, size).start()
            fields[0, chunk, row, inner] = re * factor_re - im * factor_im

    for turn in range(2):
        for block in range(len((LEADING, TRAILING)[turn])):
            forward_block(turn, block)

        @pl.when(has_partner(row_at(turn)))
        def _():
            for chunk in range(EAGER if turn == 0 else 0, CHUNKS):
                send(chunk, 1, chunk, row_at(turn)).start()

    inverse_copy.start()

    @pl.when(jnp.logical_or(me == 0, me == count - 1))
    def _():
        landed[2 * SLOTS] = jnp.zeros((NY, LANES), jnp.float32)

    def half_step(message, part, chunk, row, first_row=0, count_rows=NY):
        halo_from = 1 - row
        at = jnp.where(has_partner(row), slot(message, halo_from), 2 * SLOTS)
        other = 1 - part
        sign = jnp.float32(2 * part - 1)
        rate = factors[2, chunk, 0:1] * sign
        size = 64
        for start in range(first_row, first_row + count_rows, size):
            base = PAD + start
            center = fields[other, chunk, row, base:base + size]
            below = fields[other, chunk, row, base - 1:base - 1 + size]
            above = fields[other, chunk, row, base + 1:base + 1 + size]
            beside = fields[other, chunk, 1 - row, base:base + size]
            halo = landed[at, start:start + size]
            laplacian = (halo + beside) + (below + above) - 4.0 * center
            fields[part, chunk, row, base:base + size] += rate * laplacian

    def wait_for(message, part, chunk, row):
        @pl.when(has_partner(row))
        def _():
            send(message, 1 - part, chunk, 1 - row).wait_recv()

    def wait_sent(message, part, chunk, direction):
        @pl.when(has_partner(direction))
        def _():
            send(message, 1 - part, chunk, direction).wait_send()

    def terms_of(part, chunk, row, start, size):
        high, low = split_values(fields[part, chunk, row, pl.ds(PAD + start, size)])
        return dot(jnp.concatenate([high, low, high], axis=1), inv[chunk, part])

    def sums_of(chunk):
        return slice(2 * LANES * chunk, 2 * LANES * (chunk + 1))

    def gather_rows(part, chunk):
        for row in range(ROWS):
            for start in range(0, NY, GATHER):
                terms = terms_of(part, chunk, row, start, GATHER)
                rows = slice(start, start + GATHER)
                if part == 0:
                    out_ref[row, rows, sums_of(chunk)] = terms
                else:
                    out_ref[row, rows, sums_of(chunk)] += terms

    def advance(message, carry):
        step = message // CHUNKS
        chunk = lax.rem(message, CHUNKS)
        part = lax.rem(step, 2)

        @pl.when(step > 0)
        def _():
            for direction in range(2):
                wait_sent(message - CHUNKS, 1 - part, chunk, direction)

        for turn in range(2):
            row = row_at(turn)
            wait_for(message, part, chunk, row)
            half_step(message, part, chunk, row)

            @pl.when(has_partner(row))
            def _():
                send(message + CHUNKS, part, chunk, row).start()

        return carry

    lax.fori_loop(0, (STEPS - 2) * CHUNKS, advance, 0)
    inverse_copy.wait()

    last = STEPS * CHUNKS - 1

    def piece_copy(piece, direction):
        start, piece_rows = starts(PIECES)[piece], PIECES[piece]
        return pltpu.make_async_remote_copy(
            src_ref=fields.at[0, CHUNKS - 1, direction, pl.ds(PAD + start, piece_rows)],
            dst_ref=landed.at[slot(last, direction), pl.ds(start, piece_rows)],
            send_sem=last_send_sems.at[piece],
            recv_sem=last_recv_sems.at[piece],
            device_id=device(partner(direction)),
            device_id_type=MESH,
        )

    leaving, staying = row_at(0), row_at(1)

    for chunk in range(CHUNKS):
        message = (STEPS - 2) * CHUNKS + chunk
        for direction in range(2):
            wait_sent(message - CHUNKS, 1, chunk, direction)
        wait_for(message, 0, chunk, leaving)
        if chunk < CHUNKS - 1:
            half_step(message, 0, chunk, leaving)

            @pl.when(has_partner(leaving))
            def _():
                send(message + CHUNKS, 0, chunk, leaving).start()
        else:
            for piece in range(len(PIECES)):
                half_step(message, 0, chunk, leaving, starts(PIECES)[piece], PIECES[piece])

                @pl.when(has_partner(leaving))
                def _():
                    piece_copy(piece, leaving).start()
        wait_for(message, 0, chunk, staying)
        half_step(message, 0, chunk, staying)

        @pl.when(has_partner(staying))
        def _():
            send(message + CHUNKS, 0, chunk, staying).start()

        gather_rows(0, chunk)

    for chunk in range(CHUNKS - 1):
        message = (STEPS - 1) * CHUNKS + chunk
        for direction in range(2):
            wait_sent(message - CHUNKS, 0, chunk, direction)
        for row in (staying, leaving):
            wait_for(message, 1, chunk, row)
            half_step(message, 1, chunk, row)
        gather_rows(1, chunk)

    def finish(row, start, size):
        half_step(last, 1, CHUNKS - 1, row, start, size)
        terms = terms_of(1, CHUNKS - 1, row, start, size)
        rows = slice(start, start + size)
        out_ref[row, rows, sums_of(CHUNKS - 1)] += terms
        step = 64
        for at in range(start, start + size, step):
            rows = slice(at, at + step)
            groups = [out_ref[row, rows, lane:lane + LANES] for lane in range(0, NT, LANES)]
            whole = unfold([(groups[2 * chunk], groups[2 * chunk + 1]) for chunk in range(CHUNKS)])
            for index in range(2 * CHUNKS):
                out_ref[row, rows, index * LANES:(index + 1) * LANES] = whole[index]

    for direction in range(2):
        wait_sent(last - CHUNKS, 0, CHUNKS - 1, direction)
    wait_for(last, 1, CHUNKS - 1, staying)
    for start in range(0, NY, GATHER):
        finish(staying, start, GATHER)
    for piece in range(len(PIECES)):
        @pl.when(has_partner(leaving))
        def _():
            piece_copy(piece, 1 - leaving).wait_recv()

        finish(leaving, starts(PIECES)[piece], PIECES[piece])

    for chunk in range(CHUNKS):
        message = (STEPS - 1) * CHUNKS + chunk
        wait_sent(message, 1, chunk, staying)
        if chunk < CHUNKS - 1:
            wait_sent(message, 1, chunk, leaving)
    for piece in range(len(PIECES)):
        @pl.when(has_partner(leaving))
        def _():
            piece_copy(piece, leaving).wait_send()


def shards(narrow_size, wide_size, pressure, relax_freq, relax_depth):
    hbm = pl.BlockSpec(memory_space=pltpu.HBM)
    f32, bf16 = jnp.float32, jnp.bfloat16
    dma = pltpu.SemaphoreType.DMA
    return pl.pallas_call(
        functools.partial(step_kernel, narrow_size, wide_size),
        out_shape=pltpu.VMEM((ROWS, NY, NT), f32),
        in_specs=[hbm, hbm, hbm, hbm, hbm],
        out_specs=pl.BlockSpec(memory_space=pltpu.VMEM),
        scratch_shapes=[
            pltpu.VMEM((ROWS, NY, NT), f32),
            pltpu.VMEM((2, CHUNKS, ROWS, NY + 2 * PAD, LANES), f32),
            pltpu.VMEM((2 * SLOTS + 1, NY, LANES), f32),
            pltpu.VMEM((CHUNKS, 2, 2 * LANES, 2 * LANES), bf16),
            pltpu.VMEM((CHUNKS, 2, 3 * LANES, 2 * LANES), bf16),
            pltpu.VMEM((3, CHUNKS, 8, LANES), f32),
            pltpu.SMEM((2,), f32),
            pltpu.SMEM((2,), f32),
            dma((len(LEADING) + len(TRAILING),)),
            dma((CHUNKS + 1,)),
            dma((2,)),
            dma((2 * SLOTS,)),
            dma((2 * SLOTS,)),
            dma((len(PIECES),)),
            dma((len(PIECES),)),
        ],
        compiler_params=pltpu.CompilerParams(
            collective_id=0, has_side_effects=True, vmem_limit_bytes=59 * 2**20
        ),
        cost_estimate=pl.CostEstimate(
            flops=2 * 2 * 3 * ROWS * NY * 2 * LANES * NT, bytes_accessed=14 * 2**20, transcendentals=0
        ),
    )(relax_freq, relax_depth, pressure, jnp.asarray(forward_tables()), jnp.asarray(inverse_tables()))


def solution(mesh):
    placed = (P(("narrow", "wide"), None, None), P(), P())
    return jax.shard_map(
        functools.partial(shards, mesh.shape["narrow"], mesh.shape["wide"]),
        mesh=mesh,
        in_specs=placed,
        out_specs=P(("narrow", "wide"), None, None),
        check_vma=False,
    )
```

```python
import functools
import math

import jax
import jax.numpy as jnp
import ml_dtypes
import numpy as np
from jax import lax
from jax.experimental import pallas as pl
from jax.experimental.pallas import tpu as pltpu
from jax.sharding import PartitionSpec as P

SUBSTEPS = 3
STEPS = 2 * SUBSTEPS
WAVE_BREAKING = 0.1
RATE_TOP = 0.2

NY = 512
NT = 1024
HALF = NT // 2
LANES = 128
CHUNKS = (NT // 2) // LANES
PAD = 8
LEADING = (96, 416)
TRAILING = (512,)
GATHER = 512
PIECES = (384, 128)
EAGER = 4
SLOTS = 2 * CHUNKS
ROWS = 2
MESH = pl.DeviceIdType.MESH
ROOT_HALF = math.sqrt(0.5)


def starts(sizes):
    return [sum(sizes[:index]) for index in range(len(sizes))]


def chunk_bins(chunk):
    lane = np.arange(LANES)
    if chunk < 2:
        return 4 * lane + 2 * chunk, np.ones(LANES)
    bins = 8 * lane + 1 + 4 * (chunk - 2)
    mirrored = bins > HALF
    return np.where(mirrored, NT - bins, bins), np.where(mirrored, -1.0, 1.0)


def chunk_table(chunk):
    bins, sign = chunk_bins(chunk)
    at = np.where(sign < 0, NT - bins, bins)
    time = np.arange(2 * LANES if chunk < 2 else LANES)
    angle = 2.0 * np.pi * (time[:, None] * at[None, :] % NT) / NT
    cosine, sine = np.cos(angle), np.sin(angle)
    if chunk < 2:
        return np.concatenate([cosine, -sine], axis=1)
    return np.concatenate(
        [
            np.concatenate([cosine, -sine * sign], axis=1),
            np.concatenate([-sine, -cosine * sign], axis=1),
        ],
        axis=0,
    )


def split_table(table):
    high = table.astype(ml_dtypes.bfloat16)
    low = (table - high.astype(np.float64)).astype(ml_dtypes.bfloat16)
    return high, low


def forward_tables():
    return np.stack([np.stack(split_table(chunk_table(chunk))) for chunk in range(CHUNKS)])


def inverse_tables():
    tables = []
    for chunk in range(CHUNKS):
        weight = (np.where(chunk_bins(chunk)[0] == 0, 1.0, 2.0) / NT)[:, None]
        parts = []
        for part in range(2):
            columns = slice(part * LANES, (part + 1) * LANES)
            high, low = split_table(chunk_table(chunk)[:, columns].T * weight)
            parts.append(np.concatenate([high, high, low], axis=0))
        tables.append(np.stack(parts))
    return np.stack(tables)


def fold(groups):
    u = [groups[index] + groups[index + 4] for index in range(4)]
    v = [groups[index] - groups[index + 4] for index in range(4)]
    across = (v[1] - v[3]) * ROOT_HALF
    along = (v[1] + v[3]) * ROOT_HALF
    return (
        (u[0] + u[2], u[1] + u[3]),
        (u[0] - u[2], u[1] - u[3]),
        (v[0] + across, v[2] + along),
        (v[0] - across, v[2] - along),
    )


def unfold(sums):
    (a0, a1), (b0, b1), (p0, p1), (q0, q1) = sums
    u = (a0 + b0, a1 + b1, a0 - b0, a1 - b1)
    across, along = p0 - q0, p1 - q1
    v = (p0 + q0, (along + across) * ROOT_HALF, p1 + q1, (along - across) * ROOT_HALF)
    return [u[index] + v[index] for index in range(4)] + [u[index] - v[index] for index in range(4)]


def split_values(values):
    high = values.astype(jnp.bfloat16)
    low = (values - high.astype(jnp.float32)).astype(jnp.bfloat16)
    return high, low


def dot(lhs, rhs):
    return jnp.dot(lhs, rhs, preferred_element_type=jnp.float32)


def step_kernel(
    narrow_size, wide_size,
    freq_ref, depth_ref, pressure_ref, forward_ref, inverse_ref,
    out_ref,
    waves, fields, landed, fwd, inv, factors, freqs, depths,
    wave_sems, table_sems, scalar_sems, send_sems, recv_sems, last_send_sems, last_recv_sems,
):
    count = narrow_size * wide_size
    me = lax.axis_index("narrow") * wide_size + lax.axis_index("wide")
    core = lax.rem(me, 2)

    def device(index):
        return {"narrow": index // wide_size, "wide": lax.rem(index, wide_size)}

    def partner(direction):
        return me - 1 + 2 * direction

    def has_partner(direction):
        other = partner(direction)
        return jnp.logical_and(other >= 0, other < count)

    def row_at(turn):
        return lax.rem(core + turn, 2)

    barrier = pltpu.get_barrier_semaphore()
    for direction in range(2):
        @pl.when(has_partner(direction))
        def _():
            pl.semaphore_signal(
                barrier, inc=1, device_id=device(partner(direction)), device_id_type=MESH
            )

    def wave_copy(turn, block):
        sizes = (LEADING, TRAILING)[turn]
        rows = pl.ds(starts(sizes)[block], sizes[block])
        return pltpu.make_async_copy(
            pressure_ref.at[row_at(turn), rows],
            waves.at[row_at(turn), rows],
            wave_sems.at[turn * len(LEADING) + block],
        )

    def table_copy(chunk):
        return pltpu.make_async_copy(forward_ref.at[chunk], fwd.at[chunk], table_sems.at[chunk])

    inverse_copy = pltpu.make_async_copy(inverse_ref, inv, table_sems.at[CHUNKS])
    freq_copy = pltpu.make_async_copy(freq_ref, freqs, scalar_sems.at[0])
    depth_copy = pltpu.make_async_copy(depth_ref, depths, scalar_sems.at[1])

    freq_copy.start()
    depth_copy.start()
    wave_copy(0, 0).start()
    table_copy(0).start()
    wave_copy(0, 1).start()
    table_copy(1).start()
    for block in range(2, len(LEADING)):
        wave_copy(0, block).start()
    for chunk in range(2, CHUNKS):
        table_copy(chunk).start()
    for block in range(len(TRAILING)):
        wave_copy(1, block).start()
    zero_rows = jnp.zeros((PAD, LANES), jnp.float32)
    for part in range(2):
        for chunk in range(CHUNKS):
            for row in range(ROWS):
                fields[part, chunk, row, 0:PAD] = zero_rows
                fields[part, chunk, row, PAD + NY:] = zero_rows

    pl.semaphore_wait(
        barrier, has_partner(0).astype(jnp.int32) + has_partner(1).astype(jnp.int32)
    )

    def slot(message, direction):
        return 2 * (message % SLOTS) + direction

    def send(message, part, chunk, direction, start=0, size=NY):
        return pltpu.make_async_remote_copy(
            src_ref=fields.at[part, chunk, direction, pl.ds(PAD + start, size)],
            dst_ref=landed.at[slot(message, direction), pl.ds(start, size)],
            send_sem=send_sems.at[slot(message, direction)],
            recv_sem=recv_sems.at[slot(message, direction)],
            device_id=device(partner(direction)),
            device_id_type=MESH,
        )

    wave_copy(0, 0).wait()
    table_copy(0).wait()
    lane = lax.broadcasted_iota(jnp.int32, (8, LANES), 1)
    chunk_of = lax.broadcasted_iota(jnp.int32, (8, LANES), 0) & (CHUNKS - 1)
    counted = 8 * lane + 4 * chunk_of - 7
    odd = jnp.where(counted > HALF, NT - counted, counted)
    bins = jnp.where(chunk_of < 2, 4 * lane + 2 * chunk_of, odd).astype(jnp.float32)
    total_re = jnp.zeros_like(bins)
    total_im = jnp.zeros_like(bins)
    freq_copy.wait()
    depth_copy.wait()
    for process in range(2):
        ratio = bins / freqs[process]
        scaled = depths[process] / (1.0 + ratio * ratio)
        total_re = total_re + scaled * ratio * ratio
        total_im = total_im + scaled * ratio
    amplitude = jnp.exp(-total_re)
    rates = (
        RATE_TOP
        * jnp.minimum(bins, 1.0)
        * jnp.minimum(1.0, float(NT // 4) / jnp.maximum(bins, 1.0))
    )
    table = (amplitude * jnp.cos(total_im), -amplitude * jnp.sin(total_im), rates)
    for kind in range(3):
        for chunk in range(CHUNKS):
            factors[kind, chunk] = jnp.broadcast_to(table[kind][chunk:chunk + 1], (8, LANES))

    def forward_block(turn, block):
        row = row_at(turn)
        sizes = (LEADING, TRAILING)[turn]
        start, size = starts(sizes)[block], sizes[block]
        rows, inner = pl.ds(start, size), pl.ds(PAD + start, size)
        if turn + block > 0:
            wave_copy(turn, block).wait()
        wave = waves[row, rows]
        squared = wave * wave
        time = lax.broadcasted_iota(jnp.int32, (size, NT), 1)
        after = jnp.where(time == NT - 1, 0.0, pltpu.roll(squared, NT - 1, 1))
        before = jnp.where(time == 0, 0.0, pltpu.roll(squared, 1, 1))
        steep = wave + WAVE_BREAKING * 0.25 * (after - before)
        folded = fold([steep[:, at:at + LANES] for at in range(0, NT, LANES)])
        for chunk in range(CHUNKS):
            if turn + block == 0 and chunk > 0:
                table_copy(chunk).wait()
            high, low = split_values(jnp.concatenate(folded[chunk], axis=1))
            both = (
                dot(high, fwd[chunk, 0]) + dot(low, fwd[chunk, 0]) + dot(high, fwd[chunk, 1])
            )
            re, im = both[:, :LANES], both[:, LANES:]
            factor_re = factors[0, chunk, 0:1]
            factor_im = factors[1, chunk, 0:1]
            fields[1, chunk, row, inner] = re * factor_im + im * factor_re
            if chunk < EAGER and turn == 0:
                @pl.when(has_partner(row))
                def _():
                    send(chunk, 1, chunk, row, start, size).start()
            fields[0, chunk, row, inner] = re * factor_re - im * factor_im

    for turn in range(2):
        for block in range(len((LEADING, TRAILING)[turn])):
            forward_block(turn, block)

        @pl.when(has_partner(row_at(turn)))
        def _():
            for chunk in range(EAGER if turn == 0 else 0, CHUNKS):
                send(chunk, 1, chunk, row_at(turn)).start()

    inverse_copy.start()

    @pl.when(jnp.logical_or(me == 0, me == count - 1))
    def _():
        landed[2 * SLOTS] = jnp.zeros((NY, LANES), jnp.float32)

    def half_step(message, part, chunk, row, first_row=0, count_rows=NY):
        halo_from = 1 - row
        at = jnp.where(has_partner(row), slot(message, halo_from), 2 * SLOTS)
        other = 1 - part
        sign = jnp.float32(2 * part - 1)
        rate = factors[2, chunk, 0:1] * sign
        size = 64
        for start in range(first_row, first_row + count_rows, size):
            base = PAD + start
            center = fields[other, chunk, row, base:base + size]
            below = fields[other, chunk, row, base - 1:base - 1 + size]
            above = fields[other, chunk, row, base + 1:base + 1 + size]
            beside = fields[other, chunk, 1 - row, base:base + size]
            halo = landed[at, start:start + size]
            laplacian = (halo + beside) + (below + above) - 4.0 * center
            fields[part, chunk, row, base:base + size] += rate * laplacian

    def wait_for(message, part, chunk, row):
        @pl.when(has_partner(row))
        def _():
            send(message, 1 - part, chunk, 1 - row).wait_recv()

    def wait_sent(message, part, chunk, direction):
        @pl.when(has_partner(direction))
        def _():
            send(message, 1 - part, chunk, direction).wait_send()

    def terms_of(part, chunk, row, start, size):
        high, low = split_values(fields[part, chunk, row, pl.ds(PAD + start, size)])
        return dot(jnp.concatenate([high, low, high], axis=1), inv[chunk, part])

    def sums_of(chunk):
        return slice(2 * LANES * chunk, 2 * LANES * (chunk + 1))

    def gather_rows(part, chunk):
        for row in range(ROWS):
            for start in range(0, NY, GATHER):
                terms = terms_of(part, chunk, row, start, GATHER)
                rows = slice(start, start + GATHER)
                if part == 0:
                    out_ref[row, rows, sums_of(chunk)] = terms
                else:
                    out_ref[row, rows, sums_of(chunk)] += terms

    def advance(message, carry):
        step = message // CHUNKS
        chunk = lax.rem(message, CHUNKS)
        part = lax.rem(step, 2)

        @pl.when(step > 0)
        def _():
            for direction in range(2):
                wait_sent(message - CHUNKS, 1 - part, chunk, direction)

        for turn in range(2):
            row = row_at(turn)
            wait_for(message, part, chunk, row)
            half_step(message, part, chunk, row)

            @pl.when(has_partner(row))
            def _():
                send(message + CHUNKS, part, chunk, row).start()

        return carry

    lax.fori_loop(0, (STEPS - 2) * CHUNKS, advance, 0)
    inverse_copy.wait()

    last = STEPS * CHUNKS - 1

    def piece_copy(piece, direction):
        start, piece_rows = starts(PIECES)[piece], PIECES[piece]
        return pltpu.make_async_remote_copy(
            src_ref=fields.at[0, CHUNKS - 1, direction, pl.ds(PAD + start, piece_rows)],
            dst_ref=landed.at[slot(last, direction), pl.ds(start, piece_rows)],
            send_sem=last_send_sems.at[piece],
            recv_sem=last_recv_sems.at[piece],
            device_id=device(partner(direction)),
            device_id_type=MESH,
        )

    leaving, staying = row_at(0), row_at(1)

    for chunk in range(CHUNKS):
        message = (STEPS - 2) * CHUNKS + chunk
        for direction in range(2):
            wait_sent(message - CHUNKS, 1, chunk, direction)
        wait_for(message, 0, chunk, leaving)
        if chunk < CHUNKS - 1:
            half_step(message, 0, chunk, leaving)

            @pl.when(has_partner(leaving))
            def _():
                send(message + CHUNKS, 0, chunk, leaving).start()
        else:
            for piece in range(len(PIECES)):
                half_step(message, 0, chunk, leaving, starts(PIECES)[piece], PIECES[piece])

                @pl.when(has_partner(leaving))
                def _():
                    piece_copy(piece, leaving).start()
        wait_for(message, 0, chunk, staying)
        half_step(message, 0, chunk, staying)

        @pl.when(has_partner(staying))
        def _():
            send(message + CHUNKS, 0, chunk, staying).start()

        gather_rows(0, chunk)

    for chunk in range(CHUNKS - 1):
        message = (STEPS - 1) * CHUNKS + chunk
        for direction in range(2):
            wait_sent(message - CHUNKS, 0, chunk, direction)
        for row in (staying, leaving):
            wait_for(message, 1, chunk, row)
            half_step(message, 1, chunk, row)
        gather_rows(1, chunk)

    def finish(row, start, size):
        half_step(last, 1, CHUNKS - 1, row, start, size)
        terms = terms_of(1, CHUNKS - 1, row, start, size)
        rows = slice(start, start + size)
        out_ref[row, rows, sums_of(CHUNKS - 1)] += terms
        step = 64
        for at in range(start, start + size, step):
            rows = slice(at, at + step)
            groups = [out_ref[row, rows, lane:lane + LANES] for lane in range(0, NT, LANES)]
            whole = unfold([(groups[2 * chunk], groups[2 * chunk + 1]) for chunk in range(CHUNKS)])
            for index in range(2 * CHUNKS):
                out_ref[row, rows, index * LANES:(index + 1) * LANES] = whole[index]

    for direction in range(2):
        wait_sent(last - CHUNKS, 0, CHUNKS - 1, direction)
    wait_for(last, 1, CHUNKS - 1, staying)
    for start in range(0, NY, GATHER):
        finish(staying, start, GATHER)
    for piece in range(len(PIECES)):
        @pl.when(has_partner(leaving))
        def _():
            piece_copy(piece, 1 - leaving).wait_recv()

        finish(leaving, starts(PIECES)[piece], PIECES[piece])

    for chunk in range(CHUNKS):
        message = (STEPS - 1) * CHUNKS + chunk
        wait_sent(message, 1, chunk, staying)
        if chunk < CHUNKS - 1:
            wait_sent(message, 1, chunk, leaving)
    for piece in range(len(PIECES)):
        @pl.when(has_partner(leaving))
        def _():
            piece_copy(piece, leaving).wait_send()


def shards(narrow_size, wide_size, pressure, relax_freq, relax_depth):
    hbm = pl.BlockSpec(memory_space=pltpu.HBM)
    f32, bf16 = jnp.float32, jnp.bfloat16
    dma = pltpu.SemaphoreType.DMA
    return pl.pallas_call(
        functools.partial(step_kernel, narrow_size, wide_size),
        out_shape=pltpu.VMEM((ROWS, NY, NT), f32),
        in_specs=[hbm, hbm, hbm, hbm, hbm],
        out_specs=pl.BlockSpec(memory_space=pltpu.VMEM),
        scratch_shapes=[
            pltpu.VMEM((ROWS, NY, NT), f32),
            pltpu.VMEM((2, CHUNKS, ROWS, NY + 2 * PAD, LANES), f32),
            pltpu.VMEM((2 * SLOTS + 1, NY, LANES), f32),
            pltpu.VMEM((CHUNKS, 2, 2 * LANES, 2 * LANES), bf16),
            pltpu.VMEM((CHUNKS, 2, 3 * LANES, 2 * LANES), bf16),
            pltpu.VMEM((3, CHUNKS, 8, LANES), f32),
            pltpu.SMEM((2,), f32),
            pltpu.SMEM((2,), f32),
            dma((len(LEADING) + len(TRAILING),)),
            dma((CHUNKS + 1,)),
            dma((2,)),
            dma((2 * SLOTS,)),
            dma((2 * SLOTS,)),
            dma((len(PIECES),)),
            dma((len(PIECES),)),
        ],
        compiler_params=pltpu.CompilerParams(
            collective_id=0, has_side_effects=True, vmem_limit_bytes=59 * 2**20
        ),
        cost_estimate=pl.CostEstimate(
            flops=2 * 2 * 3 * ROWS * NY * 2 * LANES * NT, bytes_accessed=14 * 2**20, transcendentals=0
        ),
    )(relax_freq, relax_depth, pressure, jnp.asarray(forward_tables()), jnp.asarray(inverse_tables()))


def solution(mesh):
    placed = (P(("narrow", "wide"), None, None), P(), P())
    return jax.shard_map(
        functools.partial(shards, mesh.shape["narrow"], mesh.shape["wide"]),
        mesh=mesh,
        in_specs=placed,
        out_specs=P(("narrow", "wide"), None, None),
        check_vma=False,
    )
```

```python
import functools
import math

import jax
import jax.numpy as jnp
import ml_dtypes
import numpy as np
from jax import lax
from jax.experimental import pallas as pl
from jax.experimental.pallas import tpu as pltpu
from jax.sharding import PartitionSpec as P

SUBSTEPS = 3
STEPS = 2 * SUBSTEPS
WAVE_BREAKING = 0.1
RATE_TOP = 0.2

NY = 512
NT = 1024
HALF = NT // 2
LANES = 128
CHUNKS = (NT // 2) // LANES
PAD = 8
LEADING = (96, 416)
TRAILING = (512,)
GATHER = 512
PIECES = (384, 128)
EAGER = 4
SLOTS = 2 * CHUNKS
ROWS = 2
MESH = pl.DeviceIdType.MESH
ROOT_HALF = math.sqrt(0.5)


def starts(sizes):
    return [sum(sizes[:index]) for index in range(len(sizes))]


def chunk_bins(chunk):
    lane = np.arange(LANES)
    if chunk < 2:
        return 4 * lane + 2 * chunk, np.ones(LANES)
    bins = 8 * lane + 1 + 4 * (chunk - 2)
    mirrored = bins > HALF
    return np.where(mirrored, NT - bins, bins), np.where(mirrored, -1.0, 1.0)


def chunk_table(chunk):
    bins, sign = chunk_bins(chunk)
    at = np.where(sign < 0, NT - bins, bins)
    time = np.arange(2 * LANES if chunk < 2 else LANES)
    angle = 2.0 * np.pi * (time[:, None] * at[None, :] % NT) / NT
    cosine, sine = np.cos(angle), np.sin(angle)
    if chunk < 2:
        return np.concatenate([cosine, -sine], axis=1)
    return np.concatenate(
        [
            np.concatenate([cosine, -sine * sign], axis=1),
            np.concatenate([-sine, -cosine * sign], axis=1),
        ],
        axis=0,
    )


def split_table(table):
    high = table.astype(ml_dtypes.bfloat16)
    low = (table - high.astype(np.float64)).astype(ml_dtypes.bfloat16)
    return high, low


def forward_tables():
    return np.stack([np.stack(split_table(chunk_table(chunk))) for chunk in range(CHUNKS)])


def inverse_tables():
    tables = []
    for chunk in range(CHUNKS):
        weight = (np.where(chunk_bins(chunk)[0] == 0, 1.0, 2.0) / NT)[:, None]
        parts = []
        for part in range(2):
            columns = slice(part * LANES, (part + 1) * LANES)
            high, low = split_table(chunk_table(chunk)[:, columns].T * weight)
            parts.append(np.concatenate([high, high, low], axis=0))
        tables.append(np.stack(parts))
    return np.stack(tables)


def fold(groups):
    u = [groups[index] + groups[index + 4] for index in range(4)]
    v = [groups[index] - groups[index + 4] for index in range(4)]
    across = (v[1] - v[3]) * ROOT_HALF
    along = (v[1] + v[3]) * ROOT_HALF
    return (
        (u[0] + u[2], u[1] + u[3]),
        (u[0] - u[2], u[1] - u[3]),
        (v[0] + across, v[2] + along),
        (v[0] - across, v[2] - along),
    )


def unfold(sums):
    (a0, a1), (b0, b1), (p0, p1), (q0, q1) = sums
    u = (a0 + b0, a1 + b1, a0 - b0, a1 - b1)
    across, along = p0 - q0, p1 - q1
    v = (p0 + q0, (along + across) * ROOT_HALF, p1 + q1, (along - across) * ROOT_HALF)
    return [u[index] + v[index] for index in range(4)] + [u[index] - v[index] for index in range(4)]


def split_values(values):
    high = values.astype(jnp.bfloat16)
    low = (values - high.astype(jnp.float32)).astype(jnp.bfloat16)
    return high, low


def dot(lhs, rhs):
    return jnp.dot(lhs, rhs, preferred_element_type=jnp.float32)


def step_kernel(
    narrow_size, wide_size,
    freq_ref, depth_ref, pressure_ref, forward_ref, inverse_ref,
    out_ref,
    waves, fields, landed, fwd, inv, factors, freqs, depths,
    wave_sems, table_sems, scalar_sems, send_sems, recv_sems, last_send_sems, last_recv_sems,
):
    count = narrow_size * wide_size
    me = lax.axis_index("narrow") * wide_size + lax.axis_index("wide")
    core = lax.rem(me, 2)

    def device(index):
        return {"narrow": index // wide_size, "wide": lax.rem(index, wide_size)}

    def partner(direction):
        return me - 1 + 2 * direction

    def has_partner(direction):
        other = partner(direction)
        return jnp.logical_and(other >= 0, other < count)

    def row_at(turn):
        return lax.rem(core + turn, 2)

    barrier = pltpu.get_barrier_semaphore()
    for direction in range(2):
        @pl.when(has_partner(direction))
        def _():
            pl.semaphore_signal(
                barrier, inc=1, device_id=device(partner(direction)), device_id_type=MESH
            )

    def wave_copy(turn, block):
        sizes = (LEADING, TRAILING)[turn]
        rows = pl.ds(starts(sizes)[block], sizes[block])
        return pltpu.make_async_copy(
            pressure_ref.at[row_at(turn), rows],
            waves.at[row_at(turn), rows],
            wave_sems.at[turn * len(LEADING) + block],
        )

    def table_copy(chunk):
        return pltpu.make_async_copy(forward_ref.at[chunk], fwd.at[chunk], table_sems.at[chunk])

    inverse_copy = pltpu.make_async_copy(inverse_ref, inv, table_sems.at[CHUNKS])
    freq_copy = pltpu.make_async_copy(freq_ref, freqs, scalar_sems.at[0])
    depth_copy = pltpu.make_async_copy(depth_ref, depths, scalar_sems.at[1])

    freq_copy.start()
    depth_copy.start()
    wave_copy(0, 0).start()
    table_copy(0).start()
    wave_copy(0, 1).start()
    table_copy(1).start()
    for block in range(2, len(LEADING)):
        wave_copy(0, block).start()
    for chunk in range(2, CHUNKS):
        table_copy(chunk).start()
    for block in range(len(TRAILING)):
        wave_copy(1, block).start()
    zero_rows = jnp.zeros((PAD, LANES), jnp.float32)
    for part in range(2):
        for chunk in range(CHUNKS):
            for row in range(ROWS):
                fields[part, chunk, row, 0:PAD] = zero_rows
                fields[part, chunk, row, PAD + NY:] = zero_rows


    def slot(message, direction):
        return 2 * (message % SLOTS) + direction

    def send(message, part, chunk, direction, start=0, size=NY):
        return pltpu.make_async_remote_copy(
            src_ref=fields.at[part, chunk, direction, pl.ds(PAD + start, size)],
            dst_ref=landed.at[slot(message, direction), pl.ds(start, size)],
            send_sem=send_sems.at[slot(message, direction)],
            recv_sem=recv_sems.at[slot(message, direction)],
            device_id=device(partner(direction)),
            device_id_type=MESH,
        )

    wave_copy(0, 0).wait()
    table_copy(0).wait()
    lane = lax.broadcasted_iota(jnp.int32, (8, LANES), 1)
    chunk_of = lax.broadcasted_iota(jnp.int32, (8, LANES), 0) & (CHUNKS - 1)
    counted = 8 * lane + 4 * chunk_of - 7
    odd = jnp.where(counted > HALF, NT - counted, counted)
    bins = jnp.where(chunk_of < 2, 4 * lane + 2 * chunk_of, odd).astype(jnp.float32)
    total_re = jnp.zeros_like(bins)
    total_im = jnp.zeros_like(bins)
    freq_copy.wait()
    depth_copy.wait()
    for process in range(2):
        ratio = bins / freqs[process]
        scaled = depths[process] / (1.0 + ratio * ratio)
        total_re = total_re + scaled * ratio * ratio
        total_im = total_im + scaled * ratio
    amplitude = jnp.exp(-total_re)
    rates = (
        RATE_TOP
        * jnp.minimum(bins, 1.0)
        * jnp.minimum(1.0, float(NT // 4) / jnp.maximum(bins, 1.0))
    )
    table = (amplitude * jnp.cos(total_im), -amplitude * jnp.sin(total_im), rates)
    for kind in range(3):
        for chunk in range(CHUNKS):
            factors[kind, chunk] = jnp.broadcast_to(table[kind][chunk:chunk + 1], (8, LANES))

    def forward_block(turn, block):
        row = row_at(turn)
        sizes = (LEADING, TRAILING)[turn]
        start, size = starts(sizes)[block], sizes[block]
        rows, inner = pl.ds(start, size), pl.ds(PAD + start, size)
        if turn + block > 0:
            wave_copy(turn, block).wait()
        wave = waves[row, rows]
        squared = wave * wave
        time = lax.broadcasted_iota(jnp.int32, (size, NT), 1)
        after = jnp.where(time == NT - 1, 0.0, pltpu.roll(squared, NT - 1, 1))
        before = jnp.where(time == 0, 0.0, pltpu.roll(squared, 1, 1))
        steep = wave + WAVE_BREAKING * 0.25 * (after - before)
        folded = fold([steep[:, at:at + LANES] for at in range(0, NT, LANES)])
        for chunk in range(CHUNKS):
            if turn + block == 0 and chunk > 0:
                table_copy(chunk).wait()
            high, low = split_values(jnp.concatenate(folded[chunk], axis=1))
            both = (
                dot(high, fwd[chunk, 0]) + dot(low, fwd[chunk, 0]) + dot(high, fwd[chunk, 1])
            )
            re, im = both[:, :LANES], both[:, LANES:]
            factor_re = factors[0, chunk, 0:1]
            factor_im = factors[1, chunk, 0:1]
            fields[1, chunk, row, inner] = re * factor_im + im * factor_re
            if turn + block + chunk == 0:
                peers = has_partner(0).astype(jnp.int32) + has_partner(1).astype(jnp.int32)
                pl.semaphore_wait(barrier, peers)
            if chunk < EAGER and turn == 0:
                @pl.when(has_partner(row))
                def _():
                    send(chunk, 1, chunk, row, start, size).start()
            fields[0, chunk, row, inner] = re * factor_re - im * factor_im

    for turn in range(2):
        for block in range(len((LEADING, TRAILING)[turn])):
            forward_block(turn, block)

        @pl.when(has_partner(row_at(turn)))
        def _():
            for chunk in range(EAGER if turn == 0 else 0, CHUNKS):
                send(chunk, 1, chunk, row_at(turn)).start()

    inverse_copy.start()

    @pl.when(jnp.logical_or(me == 0, me == count - 1))
    def _():
        landed[2 * SLOTS] = jnp.zeros((NY, LANES), jnp.float32)

    def half_step(message, part, chunk, row, first_row=0, count_rows=NY):
        halo_from = 1 - row
        at = jnp.where(has_partner(row), slot(message, halo_from), 2 * SLOTS)
        other = 1 - part
        sign = jnp.float32(2 * part - 1)
        rate = factors[2, chunk, 0:1] * sign
        size = 64
        for start in range(first_row, first_row + count_rows, size):
            base = PAD + start
            center = fields[other, chunk, row, base:base + size]
            below = fields[other, chunk, row, base - 1:base - 1 + size]
            above = fields[other, chunk, row, base + 1:base + 1 + size]
            beside = fields[other, chunk, 1 - row, base:base + size]
            halo = landed[at, start:start + size]
            laplacian = (halo + beside) + (below + above) - 4.0 * center
            fields[part, chunk, row, base:base + size] += rate * laplacian

    def wait_for(message, part, chunk, row):
        @pl.when(has_partner(row))
        def _():
            send(message, 1 - part, chunk, 1 - row).wait_recv()

    def wait_sent(message, part, chunk, direction):
        @pl.when(has_partner(direction))
        def _():
            send(message, 1 - part, chunk, direction).wait_send()

    def terms_of(part, chunk, row, start, size):
        high, low = split_values(fields[part, chunk, row, pl.ds(PAD + start, size)])
        return dot(jnp.concatenate([high, low, high], axis=1), inv[chunk, part])

    def sums_of(chunk):
        return slice(2 * LANES * chunk, 2 * LANES * (chunk + 1))

    def gather_rows(part, chunk):
        for row in range(ROWS):
            for start in range(0, NY, GATHER):
                terms = terms_of(part, chunk, row, start, GATHER)
                rows = slice(start, start + GATHER)
                if part == 0:
                    out_ref[row, rows, sums_of(chunk)] = terms
                else:
                    out_ref[row, rows, sums_of(chunk)] += terms

    def advance(message, carry):
        step = message // CHUNKS
        chunk = lax.rem(message, CHUNKS)
        part = lax.rem(step, 2)

        @pl.when(step > 0)
        def _():
            for direction in range(2):
                wait_sent(message - CHUNKS, 1 - part, chunk, direction)

        for turn in range(2):
            row = row_at(turn)
            wait_for(message, part, chunk, row)
            half_step(message, part, chunk, row)

            @pl.when(has_partner(row))
            def _():
                send(message + CHUNKS, part, chunk, row).start()

        return carry

    lax.fori_loop(0, (STEPS - 2) * CHUNKS, advance, 0)
    inverse_copy.wait()

    last = STEPS * CHUNKS - 1

    def piece_copy(piece, direction):
        start, piece_rows = starts(PIECES)[piece], PIECES[piece]
        return pltpu.make_async_remote_copy(
            src_ref=fields.at[0, CHUNKS - 1, direction, pl.ds(PAD + start, piece_rows)],
            dst_ref=landed.at[slot(last, direction), pl.ds(start, piece_rows)],
            send_sem=last_send_sems.at[piece],
            recv_sem=last_recv_sems.at[piece],
            device_id=device(partner(direction)),
            device_id_type=MESH,
        )

    leaving, staying = row_at(0), row_at(1)

    for chunk in range(CHUNKS):
        message = (STEPS - 2) * CHUNKS + chunk
        for direction in range(2):
            wait_sent(message - CHUNKS, 1, chunk, direction)
        wait_for(message, 0, chunk, leaving)
        if chunk < CHUNKS - 1:
            half_step(message, 0, chunk, leaving)

            @pl.when(has_partner(leaving))
            def _():
                send(message + CHUNKS, 0, chunk, leaving).start()
        else:
            for piece in range(len(PIECES)):
                half_step(message, 0, chunk, leaving, starts(PIECES)[piece], PIECES[piece])

                @pl.when(has_partner(leaving))
                def _():
                    piece_copy(piece, leaving).start()
        wait_for(message, 0, chunk, staying)
        half_step(message, 0, chunk, staying)

        @pl.when(has_partner(staying))
        def _():
            send(message + CHUNKS, 0, chunk, staying).start()

        gather_rows(0, chunk)

    for chunk in range(CHUNKS - 1):
        message = (STEPS - 1) * CHUNKS + chunk
        for direction in range(2):
            wait_sent(message - CHUNKS, 0, chunk, direction)
        for row in (staying, leaving):
            wait_for(message, 1, chunk, row)
            half_step(message, 1, chunk, row)
        gather_rows(1, chunk)

    def finish(row, start, size):
        half_step(last, 1, CHUNKS - 1, row, start, size)
        terms = terms_of(1, CHUNKS - 1, row, start, size)
        rows = slice(start, start + size)
        out_ref[row, rows, sums_of(CHUNKS - 1)] += terms
        step = 64
        for at in range(start, start + size, step):
            rows = slice(at, at + step)
            groups = [out_ref[row, rows, lane:lane + LANES] for lane in range(0, NT, LANES)]
            whole = unfold([(groups[2 * chunk], groups[2 * chunk + 1]) for chunk in range(CHUNKS)])
            for index in range(2 * CHUNKS):
                out_ref[row, rows, index * LANES:(index + 1) * LANES] = whole[index]

    for direction in range(2):
        wait_sent(last - CHUNKS, 0, CHUNKS - 1, direction)
    wait_for(last, 1, CHUNKS - 1, staying)
    for start in range(0, NY, GATHER):
        finish(staying, start, GATHER)
    for piece in range(len(PIECES)):
        @pl.when(has_partner(leaving))
        def _():
            piece_copy(piece, 1 - leaving).wait_recv()

        finish(leaving, starts(PIECES)[piece], PIECES[piece])

    for chunk in range(CHUNKS):
        message = (STEPS - 1) * CHUNKS + chunk
        wait_sent(message, 1, chunk, staying)
        if chunk < CHUNKS - 1:
            wait_sent(message, 1, chunk, leaving)
    for piece in range(len(PIECES)):
        @pl.when(has_partner(leaving))
        def _():
            piece_copy(piece, leaving).wait_send()


def shards(narrow_size, wide_size, pressure, relax_freq, relax_depth):
    hbm = pl.BlockSpec(memory_space=pltpu.HBM)
    f32, bf16 = jnp.float32, jnp.bfloat16
    dma = pltpu.SemaphoreType.DMA
    return pl.pallas_call(
        functools.partial(step_kernel, narrow_size, wide_size),
        out_shape=pltpu.VMEM((ROWS, NY, NT), f32),
        in_specs=[hbm, hbm, hbm, hbm, hbm],
        out_specs=pl.BlockSpec(memory_space=pltpu.VMEM),
        scratch_shapes=[
            pltpu.VMEM((ROWS, NY, NT), f32),
            pltpu.VMEM((2, CHUNKS, ROWS, NY + 2 * PAD, LANES), f32),
            pltpu.VMEM((2 * SLOTS + 1, NY, LANES), f32),
            pltpu.VMEM((CHUNKS, 2, 2 * LANES, 2 * LANES), bf16),
            pltpu.VMEM((CHUNKS, 2, 3 * LANES, 2 * LANES), bf16),
            pltpu.VMEM((3, CHUNKS, 8, LANES), f32),
            pltpu.SMEM((2,), f32),
            pltpu.SMEM((2,), f32),
            dma((len(LEADING) + len(TRAILING),)),
            dma((CHUNKS + 1,)),
            dma((2,)),
            dma((2 * SLOTS,)),
            dma((2 * SLOTS,)),
            dma((len(PIECES),)),
            dma((len(PIECES),)),
        ],
        compiler_params=pltpu.CompilerParams(
            collective_id=0, has_side_effects=True, vmem_limit_bytes=59 * 2**20
        ),
        cost_estimate=pl.CostEstimate(
            flops=2 * 2 * 3 * ROWS * NY * 2 * LANES * NT, bytes_accessed=14 * 2**20, transcendentals=0
        ),
    )(relax_freq, relax_depth, pressure, jnp.asarray(forward_tables()), jnp.asarray(inverse_tables()))


def solution(mesh):
    placed = (P(("narrow", "wide"), None, None), P(), P())
    return jax.shard_map(
        functools.partial(shards, mesh.shape["narrow"], mesh.shape["wide"]),
        mesh=mesh,
        in_specs=placed,
        out_specs=P(("narrow", "wide"), None, None),
        check_vma=False,
    )
```

```python
import functools
import math

import jax
import jax.numpy as jnp
import ml_dtypes
import numpy as np
from jax import lax
from jax.experimental import pallas as pl
from jax.experimental.pallas import tpu as pltpu
from jax.sharding import PartitionSpec as P

SUBSTEPS = 3
STEPS = 2 * SUBSTEPS
WAVE_BREAKING = 0.1
RATE_TOP = 0.2

NY = 512
NT = 1024
HALF = NT // 2
LANES = 128
CHUNKS = (NT // 2) // LANES
PAD = 8
LEADING = (96, 416)
TRAILING = (512,)
GATHER = 512
PIECES = (384, 128)
EAGER = 4
SLOTS = 2 * CHUNKS
ROWS = 2
MESH = pl.DeviceIdType.MESH
ROOT_HALF = math.sqrt(0.5)


def starts(sizes):
    return [sum(sizes[:index]) for index in range(len(sizes))]


def chunk_bins(chunk):
    lane = np.arange(LANES)
    if chunk < 2:
        return 4 * lane + 2 * chunk, np.ones(LANES)
    bins = 8 * lane + 1 + 4 * (chunk - 2)
    mirrored = bins > HALF
    return np.where(mirrored, NT - bins, bins), np.where(mirrored, -1.0, 1.0)


def chunk_table(chunk):
    bins, sign = chunk_bins(chunk)
    at = np.where(sign < 0, NT - bins, bins)
    time = np.arange(2 * LANES if chunk < 2 else LANES)
    angle = 2.0 * np.pi * (time[:, None] * at[None, :] % NT) / NT
    cosine, sine = np.cos(angle), np.sin(angle)
    if chunk < 2:
        return np.concatenate([cosine, -sine], axis=1)
    return np.concatenate(
        [
            np.concatenate([cosine, -sine * sign], axis=1),
            np.concatenate([-sine, -cosine * sign], axis=1),
        ],
        axis=0,
    )


def split_table(table):
    high = table.astype(ml_dtypes.bfloat16)
    low = (table - high.astype(np.float64)).astype(ml_dtypes.bfloat16)
    return high, low


def forward_tables():
    return np.stack([np.stack(split_table(chunk_table(chunk))) for chunk in range(CHUNKS)])


def inverse_tables():
    tables = []
    for chunk in range(CHUNKS):
        weight = (np.where(chunk_bins(chunk)[0] == 0, 1.0, 2.0) / NT)[:, None]
        parts = []
        for part in range(2):
            columns = slice(part * LANES, (part + 1) * LANES)
            high, low = split_table(chunk_table(chunk)[:, columns].T * weight)
            parts.append(np.concatenate([high, high, low], axis=0))
        tables.append(np.stack(parts))
    return np.stack(tables)


def fold(groups):
    u = [groups[index] + groups[index + 4] for index in range(4)]
    v = [groups[index] - groups[index + 4] for index in range(4)]
    across = (v[1] - v[3]) * ROOT_HALF
    along = (v[1] + v[3]) * ROOT_HALF
    return (
        (u[0] + u[2], u[1] + u[3]),
        (u[0] - u[2], u[1] - u[3]),
        (v[0] + across, v[2] + along),
        (v[0] - across, v[2] - along),
    )


def unfold(sums):
    (a0, a1), (b0, b1), (p0, p1), (q0, q1) = sums
    u = (a0 + b0, a1 + b1, a0 - b0, a1 - b1)
    across, along = p0 - q0, p1 - q1
    v = (p0 + q0, (along + across) * ROOT_HALF, p1 + q1, (along - across) * ROOT_HALF)
    return [u[index] + v[index] for index in range(4)] + [u[index] - v[index] for index in range(4)]


def split_values(values):
    high = values.astype(jnp.bfloat16)
    low = (values - high.astype(jnp.float32)).astype(jnp.bfloat16)
    return high, low


def dot(lhs, rhs):
    return jnp.dot(lhs, rhs, preferred_element_type=jnp.float32)


def step_kernel(
    narrow_size, wide_size,
    freq_ref, depth_ref, pressure_ref, forward_ref, inverse_ref,
    out_ref,
    waves, fields, landed, fwd, inv, factors, freqs, depths,
    wave_sems, table_sems, scalar_sems, send_sems, recv_sems, last_send_sems, last_recv_sems,
):
    count = narrow_size * wide_size
    me = lax.axis_index("narrow") * wide_size + lax.axis_index("wide")
    core = lax.rem(me, 2)

    def device(index):
        return {"narrow": index // wide_size, "wide": lax.rem(index, wide_size)}

    def partner(direction):
        return me - 1 + 2 * direction

    def has_partner(direction):
        other = partner(direction)
        return jnp.logical_and(other >= 0, other < count)

    def row_at(turn):
        return lax.rem(core + turn, 2)

    barrier = pltpu.get_barrier_semaphore()
    for direction in range(2):
        @pl.when(has_partner(direction))
        def _():
            pl.semaphore_signal(
                barrier, inc=1, device_id=device(partner(direction)), device_id_type=MESH
            )

    def wave_copy(turn, block):
        sizes = (LEADING, TRAILING)[turn]
        rows = pl.ds(starts(sizes)[block], sizes[block])
        return pltpu.make_async_copy(
            pressure_ref.at[row_at(turn), rows],
            waves.at[row_at(turn), rows],
            wave_sems.at[turn * len(LEADING) + block],
        )

    def table_copy(chunk):
        chunks = pl.ds(0, 1) if chunk == 0 else pl.ds(1, CHUNKS - 1)
        return pltpu.make_async_copy(
            forward_ref.at[chunks], fwd.at[chunks], table_sems.at[min(chunk, 1)]
        )

    inverse_copy = pltpu.make_async_copy(inverse_ref, inv, table_sems.at[2])
    freq_copy = pltpu.make_async_copy(freq_ref, freqs, scalar_sems.at[0])
    depth_copy = pltpu.make_async_copy(depth_ref, depths, scalar_sems.at[1])

    freq_copy.start()
    depth_copy.start()
    wave_copy(0, 0).start()
    table_copy(0).start()
    wave_copy(0, 1).start()
    table_copy(1).start()
    for block in range(2, len(LEADING)):
        wave_copy(0, block).start()
    for block in range(len(TRAILING)):
        wave_copy(1, block).start()
    zero_rows = jnp.zeros((PAD, LANES), jnp.float32)
    for part in range(2):
        for chunk in range(CHUNKS):
            for row in range(ROWS):
                fields[part, chunk, row, 0:PAD] = zero_rows
                fields[part, chunk, row, PAD + NY:] = zero_rows

    pl.semaphore_wait(
        barrier, has_partner(0).astype(jnp.int32) + has_partner(1).astype(jnp.int32)
    )

    def slot(message, direction):
        return 2 * (message % SLOTS) + direction

    def send(message, part, chunk, direction, start=0, size=NY):
        return pltpu.make_async_remote_copy(
            src_ref=fields.at[part, chunk, direction, pl.ds(PAD + start, size)],
            dst_ref=landed.at[slot(message, direction), pl.ds(start, size)],
            send_sem=send_sems.at[slot(message, direction)],
            recv_sem=recv_sems.at[slot(message, direction)],
            device_id=device(partner(direction)),
            device_id_type=MESH,
        )

    wave_copy(0, 0).wait()
    table_copy(0).wait()
    lane = lax.broadcasted_iota(jnp.int32, (8, LANES), 1)
    chunk_of = lax.broadcasted_iota(jnp.int32, (8, LANES), 0) & (CHUNKS - 1)
    counted = 8 * lane + 4 * chunk_of - 7
    odd = jnp.where(counted > HALF, NT - counted, counted)
    bins = jnp.where(chunk_of < 2, 4 * lane + 2 * chunk_of, odd).astype(jnp.float32)
    total_re = jnp.zeros_like(bins)
    total_im = jnp.zeros_like(bins)
    freq_copy.wait()
    depth_copy.wait()
    for process in range(2):
        ratio = bins / freqs[process]
        scaled = depths[process] / (1.0 + ratio * ratio)
        total_re = total_re + scaled * ratio * ratio
        total_im = total_im + scaled * ratio
    amplitude = jnp.exp(-total_re)
    rates = (
        RATE_TOP
        * jnp.minimum(bins, 1.0)
        * jnp.minimum(1.0, float(NT // 4) / jnp.maximum(bins, 1.0))
    )
    table = (amplitude * jnp.cos(total_im), -amplitude * jnp.sin(total_im), rates)
    for kind in range(3):
        for chunk in range(CHUNKS):
            factors[kind, chunk] = jnp.broadcast_to(table[kind][chunk:chunk + 1], (8, LANES))

    def forward_block(turn, block):
        row = row_at(turn)
        sizes = (LEADING, TRAILING)[turn]
        start, size = starts(sizes)[block], sizes[block]
        rows, inner = pl.ds(start, size), pl.ds(PAD + start, size)
        if turn + block > 0:
            wave_copy(turn, block).wait()
        wave = waves[row, rows]
        squared = wave * wave
        time = lax.broadcasted_iota(jnp.int32, (size, NT), 1)
        after = jnp.where(time == NT - 1, 0.0, pltpu.roll(squared, NT - 1, 1))
        before = jnp.where(time == 0, 0.0, pltpu.roll(squared, 1, 1))
        steep = wave + WAVE_BREAKING * 0.25 * (after - before)
        folded = fold([steep[:, at:at + LANES] for at in range(0, NT, LANES)])
        for chunk in range(CHUNKS):
            if turn + block == 0 and chunk == 1:
                table_copy(chunk).wait()
            high, low = split_values(jnp.concatenate(folded[chunk], axis=1))
            both = (
                dot(high, fwd[chunk, 0]) + dot(low, fwd[chunk, 0]) + dot(high, fwd[chunk, 1])
            )
            re, im = both[:, :LANES], both[:, LANES:]
            factor_re = factors[0, chunk, 0:1]
            factor_im = factors[1, chunk, 0:1]
            fields[1, chunk, row, inner] = re * factor_im + im * factor_re
            if chunk < EAGER and turn == 0:
                @pl.when(has_partner(row))
                def _():
                    send(chunk, 1, chunk, row, start, size).start()
            fields[0, chunk, row, inner] = re * factor_re - im * factor_im

    for turn in range(2):
        for block in range(len((LEADING, TRAILING)[turn])):
            forward_block(turn, block)

        @pl.when(has_partner(row_at(turn)))
        def _():
            for chunk in range(EAGER if turn == 0 else 0, CHUNKS):
                send(chunk, 1, chunk, row_at(turn)).start()

    inverse_copy.start()

    @pl.when(jnp.logical_or(me == 0, me == count - 1))
    def _():
        landed[2 * SLOTS] = jnp.zeros((NY, LANES), jnp.float32)

    def half_step(message, part, chunk, row, first_row=0, count_rows=NY):
        halo_from = 1 - row
        at = jnp.where(has_partner(row), slot(message, halo_from), 2 * SLOTS)
        other = 1 - part
        sign = jnp.float32(2 * part - 1)
        rate = factors[2, chunk, 0:1] * sign
        size = 64
        for start in range(first_row, first_row + count_rows, size):
            base = PAD + start
            center = fields[other, chunk, row, base:base + size]
            below = fields[other, chunk, row, base - 1:base - 1 + size]
            above = fields[other, chunk, row, base + 1:base + 1 + size]
            beside = fields[other, chunk, 1 - row, base:base + size]
            halo = landed[at, start:start + size]
            laplacian = (halo + beside) + (below + above) - 4.0 * center
            fields[part, chunk, row, base:base + size] += rate * laplacian

    def wait_for(message, part, chunk, row):
        @pl.when(has_partner(row))
        def _():
            send(message, 1 - part, chunk, 1 - row).wait_recv()

    def wait_sent(message, part, chunk, direction):
        @pl.when(has_partner(direction))
        def _():
            send(message, 1 - part, chunk, direction).wait_send()

    def terms_of(part, chunk, row, start, size):
        high, low = split_values(fields[part, chunk, row, pl.ds(PAD + start, size)])
        return dot(jnp.concatenate([high, low, high], axis=1), inv[chunk, part])

    def sums_of(chunk):
        return slice(2 * LANES * chunk, 2 * LANES * (chunk + 1))

    def gather_rows(part, chunk):
        for row in range(ROWS):
            for start in range(0, NY, GATHER):
                terms = terms_of(part, chunk, row, start, GATHER)
                rows = slice(start, start + GATHER)
                if part == 0:
                    out_ref[row, rows, sums_of(chunk)] = terms
                else:
                    out_ref[row, rows, sums_of(chunk)] += terms

    def advance(message, carry):
        step = message // CHUNKS
        chunk = lax.rem(message, CHUNKS)
        part = lax.rem(step, 2)

        @pl.when(step > 0)
        def _():
            for direction in range(2):
                wait_sent(message - CHUNKS, 1 - part, chunk, direction)

        for turn in range(2):
            row = row_at(turn)
            wait_for(message, part, chunk, row)
            half_step(message, part, chunk, row)

            @pl.when(has_partner(row))
            def _():
                send(message + CHUNKS, part, chunk, row).start()

        return carry

    lax.fori_loop(0, (STEPS - 2) * CHUNKS, advance, 0)
    inverse_copy.wait()

    last = STEPS * CHUNKS - 1

    def piece_copy(piece, direction):
        start, piece_rows = starts(PIECES)[piece], PIECES[piece]
        return pltpu.make_async_remote_copy(
            src_ref=fields.at[0, CHUNKS - 1, direction, pl.ds(PAD + start, piece_rows)],
            dst_ref=landed.at[slot(last, direction), pl.ds(start, piece_rows)],
            send_sem=last_send_sems.at[piece],
            recv_sem=last_recv_sems.at[piece],
            device_id=device(partner(direction)),
            device_id_type=MESH,
        )

    leaving, staying = row_at(0), row_at(1)

    for chunk in range(CHUNKS):
        message = (STEPS - 2) * CHUNKS + chunk
        for direction in range(2):
            wait_sent(message - CHUNKS, 1, chunk, direction)
        wait_for(message, 0, chunk, leaving)
        if chunk < CHUNKS - 1:
            half_step(message, 0, chunk, leaving)

            @pl.when(has_partner(leaving))
            def _():
                send(message + CHUNKS, 0, chunk, leaving).start()
        else:
            for piece in range(len(PIECES)):
                half_step(message, 0, chunk, leaving, starts(PIECES)[piece], PIECES[piece])

                @pl.when(has_partner(leaving))
                def _():
                    piece_copy(piece, leaving).start()
        wait_for(message, 0, chunk, staying)
        half_step(message, 0, chunk, staying)

        @pl.when(has_partner(staying))
        def _():
            send(message + CHUNKS, 0, chunk, staying).start()

        gather_rows(0, chunk)

    for chunk in range(CHUNKS - 1):
        message = (STEPS - 1) * CHUNKS + chunk
        for direction in range(2):
            wait_sent(message - CHUNKS, 0, chunk, direction)
        for row in (staying, leaving):
            wait_for(message, 1, chunk, row)
            half_step(message, 1, chunk, row)
        gather_rows(1, chunk)

    def finish(row, start, size):
        half_step(last, 1, CHUNKS - 1, row, start, size)
        terms = terms_of(1, CHUNKS - 1, row, start, size)
        rows = slice(start, start + size)
        out_ref[row, rows, sums_of(CHUNKS - 1)] += terms
        step = 64
        for at in range(start, start + size, step):
            rows = slice(at, at + step)
            groups = [out_ref[row, rows, lane:lane + LANES] for lane in range(0, NT, LANES)]
            whole = unfold([(groups[2 * chunk], groups[2 * chunk + 1]) for chunk in range(CHUNKS)])
            for index in range(2 * CHUNKS):
                out_ref[row, rows, index * LANES:(index + 1) * LANES] = whole[index]

    for direction in range(2):
        wait_sent(last - CHUNKS, 0, CHUNKS - 1, direction)
    wait_for(last, 1, CHUNKS - 1, staying)
    for start in range(0, NY, GATHER):
        finish(staying, start, GATHER)
    for piece in range(len(PIECES)):
        @pl.when(has_partner(leaving))
        def _():
            piece_copy(piece, 1 - leaving).wait_recv()

        finish(leaving, starts(PIECES)[piece], PIECES[piece])

    for chunk in range(CHUNKS):
        message = (STEPS - 1) * CHUNKS + chunk
        wait_sent(message, 1, chunk, staying)
        if chunk < CHUNKS - 1:
            wait_sent(message, 1, chunk, leaving)
    for piece in range(len(PIECES)):
        @pl.when(has_partner(leaving))
        def _():
            piece_copy(piece, leaving).wait_send()


def shards(narrow_size, wide_size, pressure, relax_freq, relax_depth):
    hbm = pl.BlockSpec(memory_space=pltpu.HBM)
    f32, bf16 = jnp.float32, jnp.bfloat16
    dma = pltpu.SemaphoreType.DMA
    return pl.pallas_call(
        functools.partial(step_kernel, narrow_size, wide_size),
        out_shape=pltpu.VMEM((ROWS, NY, NT), f32),
        in_specs=[hbm, hbm, hbm, hbm, hbm],
        out_specs=pl.BlockSpec(memory_space=pltpu.VMEM),
        scratch_shapes=[
            pltpu.VMEM((ROWS, NY, NT), f32),
            pltpu.VMEM((2, CHUNKS, ROWS, NY + 2 * PAD, LANES), f32),
            pltpu.VMEM((2 * SLOTS + 1, NY, LANES), f32),
            pltpu.VMEM((CHUNKS, 2, 2 * LANES, 2 * LANES), bf16),
            pltpu.VMEM((CHUNKS, 2, 3 * LANES, 2 * LANES), bf16),
            pltpu.VMEM((3, CHUNKS, 8, LANES), f32),
            pltpu.SMEM((2,), f32),
            pltpu.SMEM((2,), f32),
            dma((len(LEADING) + len(TRAILING),)),
            dma((3,)),
            dma((2,)),
            dma((2 * SLOTS,)),
            dma((2 * SLOTS,)),
            dma((len(PIECES),)),
            dma((len(PIECES),)),
        ],
        compiler_params=pltpu.CompilerParams(
            collective_id=0, has_side_effects=True, vmem_limit_bytes=59 * 2**20
        ),
        cost_estimate=pl.CostEstimate(
            flops=2 * 2 * 3 * ROWS * NY * 2 * LANES * NT, bytes_accessed=14 * 2**20, transcendentals=0
        ),
    )(relax_freq, relax_depth, pressure, jnp.asarray(forward_tables()), jnp.asarray(inverse_tables()))


def solution(mesh):
    placed = (P(("narrow", "wide"), None, None), P(), P())
    return jax.shard_map(
        functools.partial(shards, mesh.shape["narrow"], mesh.shape["wide"]),
        mesh=mesh,
        in_specs=placed,
        out_specs=P(("narrow", "wide"), None, None),
        check_vma=False,
    )
```
